128 devices in a mesh: face: 8 (over x_lo, y), tile: 16 (over x_hi, z, core).
Axes of the slice: x: 4 (x_hi: 2, x_lo: 2; x = x_hi * 2 + x_lo), y: 4, z: 4, core: 2. Of those that a mesh axis runs over, the one named last changes fastest.
Arguments:
- checkpoint: bfloat16 [48, 32768], P(None, 'tile'), may hold values from -6 to 6
- remap_weights: bfloat16 [8, 16, 16, 256, 1024], P('face', 'tile'), may hold values from -0.09375 to 0.09375
- margins: int32 [8, 16, 16], P('face', 'tile'), may hold values from 0 to 127, as said below
- seams: int32 [8, 16, 3, 4], P('face', 'tile'), may hold values from 0 to 127, as said below
- rotation_angle: float32 [8, 16, 1024], P('face', 'tile'), may hold values from -3.140625 to 3.140625
Outputs:
- scalars: bfloat16 [8, 16, 32, 1024], P('face', 'tile')
- dgrid_winds: bfloat16 [8, 16, 16, 1024], P('face', 'tile')
- vorticity: float32 [8, 16, 8, 1024], P('face', 'tile')
The draws below stay inside these ranges and needn't reach their ends.
Inputs may be any that keep to these rules, and one draw needn't show every extreme that they name: `margins`: each tile lists 16 block ids in rising order; entries 2 m to 2 m + 1 lie in the blocks of one reader (id // 8), a different reader for each m, so every tile takes exactly 2 blocks from each of 8 readers. seams[f, g, 0, e] is the number f2 16 + g2 of the tile across edge e, seams[f, g, 1, e] the edge of that tile, seams[f, g, 2, e] is 1 where the two rims run opposite ways and 0 else; the pairing is symmetric with equal flags, and the four tiles across one tile's edges are four different tiles, none of them the tile itself.
All inputs are finite; a program needn't handle non-finite values.
Results may differ from the reference program's by a relative error of at most 0.001.
Values may be sent and summed in bfloat16 or wider, within the bound.
No kernel may reach another device: no remote copies, remote signals or barrier semaphores. Data moves between devices by JAX's collectives and lax.ppermute only.
A program may use at most 64 MiB of HBM per device.

```python
import jax
import jax.numpy as jnp
from jax import lax

LEV = 8
FIELDS = 6
TS = 32
SB = 256
BLK_DEV = 8
K = 16
CAP = 2
SMOOTH = 2
NBLK = 128
N_FACE = 8
N_TILE = 16


def draw_margins(key, part):
    key = jax.random.fold_in(key, 11)
    tile_count = N_FACE * N_TILE
    groups = K // CAP
    subkeys = jax.random.split(key, 4)
    reader_perm = jax.vmap(lambda subkey: jax.random.permutation(subkey, N_TILE))(jax.random.split(subkeys[0], tile_count))
    readers = jnp.sort(reader_perm[:, :groups], axis=1)
    block_perm = jax.vmap(lambda subkey: jax.random.permutation(subkey, BLK_DEV))(jax.random.split(subkeys[1], tile_count * groups))
    within = jnp.sort(block_perm.reshape(tile_count, groups, BLK_DEV)[:, :, :CAP], axis=2)
    top_tile = jax.random.randint(subkeys[2], (), 0, tile_count)
    low_tile = jax.random.randint(subkeys[3], (), 0, tile_count)
    tile_rows = jnp.arange(tile_count)[:, None]
    group_index = jnp.arange(groups)[None, :]
    readers = jnp.where((tile_rows == top_tile) & (group_index == groups - 1), N_TILE - 1, readers)
    readers = jnp.where((tile_rows == low_tile) & (group_index == 0), 0, readers)
    slot_index = jnp.arange(CAP)[None, None, :]
    tile_cube = jnp.arange(tile_count)[:, None, None]
    group_cube = jnp.arange(groups)[None, :, None]
    within = jnp.where((tile_cube == top_tile) & (group_cube == groups - 1) & (slot_index == CAP - 1), BLK_DEV - 1, within)
    within = jnp.where((tile_cube == low_tile) & (group_cube == 0) & (slot_index == 0), 0, within)
    block_ids = readers[:, :, None] * BLK_DEV + within
    return block_ids.reshape(N_FACE, N_TILE, K).astype(jnp.int32)


def draw_seams(key, part):
    key = jax.random.fold_in(key, 23)
    tile_count = N_FACE * N_TILE
    order_key, first_key, second_key = jax.random.split(key, 3)
    order = jax.random.permutation(order_key, tile_count).astype(jnp.int32)
    flip_near = jax.random.randint(first_key, (tile_count,), 0, 2).astype(jnp.int32)
    flip_far = jax.random.randint(second_key, (tile_count,), 0, 2).astype(jnp.int32)
    position = jnp.arange(tile_count, dtype=jnp.int32)
    after_one = order[(position + 1) % tile_count]
    before_one = order[(position - 1) % tile_count]
    after_two = order[(position + 2) % tile_count]
    before_two = order[(position - 2) % tile_count]
    partners = jnp.stack([after_one, after_two, before_one, before_two], axis=1)
    partner_edges = jnp.broadcast_to(jnp.array([2, 3, 0, 1], jnp.int32)[None, :], (tile_count, 4))
    flags = jnp.stack([flip_near, flip_far, flip_near[(position - 1) % tile_count], flip_far[(position - 2) % tile_count]], axis=1)
    by_position = jnp.stack([partners, partner_edges, flags], axis=1)
    table = jnp.zeros((tile_count, 3, 4), jnp.int32).at[order].set(by_position)
    return table.reshape(N_FACE, N_TILE, 3, 4).astype(jnp.int32)


def level_of(own_key, dims, pieces, least, largest):
    level = 1.0
    for dim, shards_of in pieces:
        draws = jax.random.uniform(jax.random.fold_in(jax.random.fold_in(own_key, 6), dim), (shards_of,), jnp.float32, least / len(pieces), largest / len(pieces))
        level = level * jnp.repeat(jnp.exp(draws), dims[dim] // shards_of).reshape((-1,) + (1,) * (len(dims) - 1 - dim))
    return level


def centred(key, dims, scale, bound, shards=(), kind=jnp.bfloat16):
    gain = level_of(key, dims, shards, -0.22, 0.18) if shards else 1.0
    values = jax.random.normal(key, dims, jnp.float32) * scale * gain
    return jnp.minimum(jnp.maximum(values, -bound), bound).astype(kind)


def setup_inputs(seed: int = 0) -> dict:
    key_list = jax.random.split(jax.random.key(seed), 6)
    checkpoint = centred(key_list[0], (FIELDS * LEV, SB * NBLK), 1.0, 6.0, ((1, 16),))
    remap_weights = centred(key_list[1], (N_FACE, N_TILE, K, SB, TS * TS), (K * SB) ** -0.5, 0.09375, ((0, 8), (1, 16)))
    margins = draw_margins(jax.random.fold_in(key_list[5], 71), 0)
    seams = draw_seams(jax.random.fold_in(key_list[5], 71), 0)
    rotation_angle = jnp.clip(jax.random.uniform(key_list[4], (N_FACE, N_TILE, TS * TS), jnp.float32, -3.140625, 3.140625), -3.140625, 3.140625)
    return {"checkpoint": checkpoint, "remap_weights": remap_weights, "margins": margins, "seams": seams, "rotation_angle": rotation_angle}


def edge_rims(grid_field):
    return jnp.stack([grid_field[:, -1, :], grid_field[:, :, -1], grid_field[:, 0, :], grid_field[:, :, 0]], axis=0)


def neighbours(gathered, seam_table):
    slot_index = seam_table[0] * 4 + seam_table[1]
    picked = jnp.take(gathered, slot_index, axis=0)
    return jnp.where((seam_table[2] == 1)[:, None, None], jnp.flip(picked, axis=-1), picked)


def shifted(grid_field, halo_rims):
    plus_x = jnp.concatenate([grid_field[:, :, 1:], halo_rims[1][:, :, None]], axis=2)
    minus_x = jnp.concatenate([halo_rims[3][:, :, None], grid_field[:, :, :-1]], axis=2)
    plus_y = jnp.concatenate([grid_field[:, 1:, :], halo_rims[0][:, None, :]], axis=1)
    minus_y = jnp.concatenate([halo_rims[2][:, None, :], grid_field[:, :-1, :]], axis=1)
    return plus_x, minus_x, plus_y, minus_y


def dgrid_and_curl(wind_field, plus_x, minus_x, plus_y, minus_y, angle):
    wind_levels = wind_field.shape[0] // 2
    cosine = jnp.cos(angle)
    sine_part = jnp.sin(angle)
    eastward = wind_field[:wind_levels]
    northward = wind_field[wind_levels:]
    along_edge = cosine * (0.5 * (eastward + plus_y[:wind_levels])) + sine_part * (0.5 * (northward + plus_y[wind_levels:]))
    across = -sine_part * (0.5 * (eastward + plus_x[:wind_levels])) + cosine * (0.5 * (northward + plus_x[wind_levels:]))
    curl_field = cosine * (0.5 * (plus_x[wind_levels:] - minus_x[wind_levels:]) - 0.5 * (plus_y[:wind_levels] - minus_y[:wind_levels]))
    curl_field = curl_field - sine_part * (0.5 * (plus_x[:wind_levels] - minus_x[:wind_levels]) + 0.5 * (plus_y[wind_levels:] - minus_y[wind_levels:]))
    return jnp.concatenate([along_edge, across], axis=0), curl_field


def smooth_once(vortex, plus_x, minus_x, plus_y, minus_y):
    return vortex + 0.2 * (plus_x + minus_x + plus_y + minus_y - 4.0 * vortex)


def reference(checkpoint, remap_weights, margins, seams, rotation_angle):
    tile_count = N_FACE * N_TILE
    channels = checkpoint.shape[0]
    blocks = checkpoint.reshape(channels, NBLK, SB)
    weights = remap_weights.reshape(tile_count, K * SB, TS * TS)
    wanted = margins.reshape(tile_count, K)

    def remap_tile(inputs):
        tile_weights, block_ids = inputs
        chosen = jnp.take(blocks, block_ids, axis=1).reshape(channels, K * SB)
        return jnp.dot(chosen, tile_weights, preferred_element_type=jnp.float32)

    remapped = lax.map(remap_tile, (weights, wanted))
    scalars = remapped[:, 2 * LEV:].astype(jnp.bfloat16)
    wind_field = remapped[:, :2 * LEV].reshape(tile_count, 2 * LEV, TS, TS)
    tables = seams.reshape(tile_count, 3, 4)
    angles = rotation_angle.reshape(tile_count, TS, TS)

    def with_halos(grid_field):
        gathered = jax.vmap(edge_rims)(grid_field)
        gathered = gathered.reshape(tile_count * 4, grid_field.shape[1], TS)
        halo_rims = jax.vmap(neighbours, in_axes=(None, 0))(gathered, tables)
        return jax.vmap(shifted)(grid_field, halo_rims)

    wind_shifts = with_halos(wind_field)
    dgrid, vortex = jax.vmap(dgrid_and_curl)(wind_field, wind_shifts[0], wind_shifts[1], wind_shifts[2], wind_shifts[3], angles)
    for repeat in range(SMOOTH):
        vort_shifts = with_halos(vortex)
        vortex = jax.vmap(smooth_once)(vortex, vort_shifts[0], vort_shifts[1], vort_shifts[2], vort_shifts[3])
    scalars = scalars.reshape(N_FACE, N_TILE, (FIELDS - 2) * LEV, TS * TS)
    dgrid = dgrid.astype(jnp.bfloat16).reshape(N_FACE, N_TILE, 2 * LEV, TS * TS)
    vortex = vortex.reshape(N_FACE, N_TILE, LEV, TS * TS)
    return scalars, dgrid, vortex
```

```python
import jax
import jax.numpy as jnp
from jax import lax
from jax.experimental import pallas as pl
from jax.experimental.pallas import tpu as pltpu
from jax.sharding import PartitionSpec as P

LEV = 8
FIELDS = 6
TS = 32
CELLS = TS * TS
SB = 256
BLK_DEV = 8
K = 16
CAP = 2
GROUPS = K // CAP
N_TILE = 16
TILES = 128
ROWS = FIELDS * LEV
WINDS = 2 * LEV
LANES = 128
MIB = 1 << 20
HEAD = 1024
CHUNK = 512
F32 = jnp.float32
BF16 = jnp.bfloat16


def iota(shape, dim):
    return lax.broadcasted_iota(jnp.int32, shape, dim)


def dot(a, b, contract=((1,), (0,))):
    return lax.dot_general(a, b, (contract, ((), ())), preferred_element_type=F32)


def halves(x):
    hi = x.astype(BF16).astype(F32)
    return hi, x - hi


def roll(x, shift):
    return pltpu.roll(x, shift % x.shape[1], 1)


def lane_pick(group, values):
    out = jnp.full(group.shape, values[0])
    for index in range(1, len(values)):
        out = jnp.where(group == index, values[index], out)
    return out


def towards(direction, cosine, sine, d_east, d_north):
    a_east = jnp.where(
        direction == 0, -cosine, jnp.where(direction == 1, -sine, jnp.where(direction == 2, cosine, sine))
    )
    a_north = jnp.where(
        direction == 0, -sine, jnp.where(direction == 1, cosine, jnp.where(direction == 2, sine, -cosine))
    )
    return 0.5 * (a_east * d_east + a_north * d_north)


def neighbours_within(h, row, col):
    return (
        jnp.where(col == TS - 1, h, roll(h, -1)),
        jnp.where(col == 0, h, roll(h, 1)),
        jnp.where(row == TS - 1, h, roll(h, -TS)),
        jnp.where(row == 0, h, roll(h, TS)),
    )


def ask_kernel(margins_ref, out_ref, margins, sem):
    copy = pltpu.make_async_copy(margins_ref, margins, sem)
    copy.start()
    copy.wait()
    reader, lane = iota((N_TILE, LANES), 0), iota((N_TILE, LANES), 1)
    asked = jnp.zeros((N_TILE, LANES), jnp.int32)
    for m in range(GROUPS):
        first, second = margins[CAP * m], margins[CAP * m + 1]
        asked = jnp.where(reader == (first >> 3), jnp.where(lane == 0, first, second), asked)
    asked = asked & (BLK_DEV - 1)
    for r in range(N_TILE):
        out_ref[r] = asked[r : r + 1]


def prepare_kernel(
    margins_ref, seams_ref, held_ref, meta_ref, held_out, sem
):
    copy = pltpu.make_async_copy(held_ref, held_out, sem)
    copy.start()

    level, lane = iota((LEV, LANES), 0), iota((LEV, LANES), 1)
    meta = jnp.zeros((LEV, LANES), jnp.int32)
    for m in range(GROUPS):
        reader = jnp.clip(margins_ref[CAP * m] >> 3, 0, N_TILE - 1)
        meta = jnp.where((level == 0) & (lane == m), reader, meta)
    for kind in range(3):
        for e in range(4):
            meta = jnp.where((level == kind + 1) & (lane == e), seams_ref[kind, e], meta)
    meta_ref[...] = meta
    copy.wait()


def select_kernel(asked_ref, held_ref, out_ref, sem):
    copies = []
    for g in range(N_TILE):
        for j in range(CAP):
            block = asked_ref[g, j] & (BLK_DEV - 1)
            copies.append(
                pltpu.make_async_copy(
                    held_ref.at[:, pl.ds(pl.multiple_of(block * SB, SB), SB)],
                    out_ref.at[g, :, pl.ds(j * SB, SB)],
                    sem.at[g, j],
                )
            )
    for copy in copies:
        copy.start()
    for copy in copies:
        copy.wait()


def fetch_kernel(weights_ref, asked_ref, head_ref, sem):
    copy = pltpu.make_async_copy(weights_ref.at[pl.ds(0, HEAD)], head_ref, sem)
    copy.start()
    copy.wait()


def remap_kernel(
    meta_ref, blocks_ref, head_ref, weights_ref, angle_ref,
    scalars_ref, wind_ref, trig_ref, place_ref, send_ref,
    chosen, streamed, pick_ref, scalars_out, sems, out_sem,
):
    spans = [(k, pl.ds(k, CHUNK)) for k in range(HEAD, K * SB, CHUNK)]
    copies = [
        pltpu.make_async_copy(weights_ref.at[span], streamed.at[pl.ds(k - HEAD, CHUNK)], sems.at[index])
        for index, (k, span) in enumerate(spans)
    ]
    for copy in copies:
        copy.start()
    for m in range(GROUPS):
        chosen[:, CAP * SB * m : CAP * SB * (m + 1)] = blocks_ref[meta_ref[0, m]]
    total = dot(chosen[:, :HEAD], head_ref[...])

    angle = angle_ref[...]
    trig_ref[...] = jnp.where((iota((LEV, CELLS), 0) & 1) == 0, jnp.cos(angle), jnp.sin(angle))

    lane = iota((1, 3 * LANES), 1)
    edge, depth, at = (lane >> 6) & 3, (lane >> 5) & 1, lane & 31
    rim_cell = jnp.where(
        edge == 0, (TS - 1 - depth) * TS + at,
        jnp.where(edge == 1, at * TS + TS - 1 - depth, jnp.where(edge == 2, depth * TS + at, at * TS + depth)),
    )
    corner, k = (lane >> 2) & 3, lane & 3
    c_row, c_col = (corner >> 1) * (TS - 1), (corner & 1) * (TS - 1)
    c_row = jnp.where(k == 2, jnp.where(c_row == 0, 1, TS - 2), c_row)
    c_col = jnp.where(k == 1, jnp.where(c_col == 0, 1, TS - 2), c_col)
    corner_cell = jnp.where((lane & 127) >= 96, c_row * TS + c_col, -1)
    taken = jnp.where(lane < 2 * LANES, rim_cell, corner_cell)
    pick_ref[...] = (iota((CELLS, 3 * LANES), 0) == taken).astype(F32).astype(BF16)

    line = iota((LANES, 1), 0)
    line_edge, line_at = line >> 5, line & 31
    flipped = lane_pick(line_edge, [meta_ref[3, e] for e in range(4)]) == 1
    line_at = jnp.where(flipped, TS - 1 - line_at, line_at)
    rim_cell = jnp.where(
        line_edge == 0, (TS - 1) * TS + line_at,
        jnp.where(line_edge == 1, line_at * TS + TS - 1, jnp.where(line_edge == 2, line_at, line_at * TS)),
    )
    place_ref[...] = (iota((LANES, CELLS), 1) == rim_cell).astype(F32).astype(BF16)

    for copy, (k, _) in zip(copies, spans):
        copy.wait()
        total = total + dot(chosen[:, k : k + CHUNK], streamed[k - HEAD : k - HEAD + CHUNK])
    scalars_out[...] = total[WINDS:].astype(BF16)
    out_copy = pltpu.make_async_copy(scalars_out, scalars_ref, out_sem)
    out_copy.start()
    wind = total[:WINDS]
    wind_ref[...] = wind
    east, north = wind[:LEV], wind[LEV:]

    cell = iota((1, CELLS), 1)
    row, col = cell >> 5, cell & (TS - 1)
    trig = trig_ref[...]
    cosine, sine = trig[0:1], trig[1:2]
    ex, exm, ey, eym = neighbours_within(east, row, col)
    nx, nxm, ny, nym = neighbours_within(north, row, col)
    curl = cosine * (0.5 * (nx - nxm) - 0.5 * (ey - eym)) - sine * (0.5 * (ex - exm) + 0.5 * (ny - nym))

    hi, lo = halves(jnp.concatenate([east, north, curl, trig], axis=0))
    got = dot(jnp.concatenate([hi, lo], axis=0).astype(BF16), pick_ref[...])

    lane = iota((LEV, LANES), 1)
    level = iota((LEV, LANES), 0)
    group = lane >> 5
    corners = got[:, 2 * LANES :]
    common_top = jnp.where((level == 5) | (level == 6), corners[24:32], 0.0)
    for e in range(4):
        tile = meta_ref[1, e].astype(F32)
        code = (meta_ref[2, e] * 2 + meta_ref[3, e]).astype(F32)
        common_top = jnp.where((level == 4) & (lane == 96 + e), tile, common_top)
        common_top = jnp.where((level == 4) & (lane == 100 + e), code, common_top)
    common_low = jnp.where(
        lane >= 112, corners[8:16], jnp.where((lane & 3) == 3, corners[16:24], corners[0:8])
    )
    common_low = jnp.where(group == 3, common_low, 0.0)
    common = jnp.concatenate([common_top, common_low], axis=0).astype(BF16)
    for t in range(TILES):
        send_ref[t] = common
    for e in range(4):
        rim = roll(got[:, LANES * (e // 2) : LANES * (e // 2 + 1)], -64 * (e % 2))
        top = jnp.where(
            group == 0, rim[0:8],
            jnp.where(group == 1, roll(rim[32:40], 32), jnp.where(group == 2, roll(rim[16:24], 64), common_top)),
        )
        top = jnp.where((group == 3) & (level < 2), roll(rim[24:32], 96), top)
        top = jnp.where((group == 3) & ((level == 2) | (level == 3)), roll(rim[24:32], 64), top)
        low = jnp.where(
            group == 0, rim[8:16],
            jnp.where(group == 1, roll(rim[40:48], 32), jnp.where(group == 2, roll(rim[16:24], 32), common_low)),
        )
        send_ref[jnp.clip(meta_ref[1, e], 0, TILES - 1)] = jnp.concatenate([top, low], axis=0).astype(BF16)
    out_copy.wait()


def smooth_kernel(
    meta_ref, packets_ref, wind_ref, trig_ref, place_ref, dgrid_ref, vortex_ref,
):
    def packet(tile):
        both = packets_ref[tile].astype(F32)
        return both[:LEV], both[LEV:]

    def corner_of(edge, end):
        return jnp.where((edge & 1) == 0, jnp.where(edge == 0, 2, 0) + end, 2 * end + jnp.where(edge == 1, 1, 0))

    lane = iota((LEV, LANES), 1)
    level = iota((LEV, LANES), 0)
    group = lane >> 5
    at = lane & 31
    zero = jnp.zeros((LEV, LANES), F32)
    edges = [meta_ref[2, e] for e in range(4)]
    near = [packet(jnp.clip(meta_ref[1, e], 0, TILES - 1)) for e in range(4)]

    def strip(half, source):
        out = roll(near[0][half], -32 * source)
        for e in range(1, 4):
            out = jnp.where(group == e, roll(near[e][half], 32 * (e - source)), out)
        return out

    east_hi, east_lo, c0, misc = [strip(0, s) for s in range(4)]
    north_hi, north_lo, c1 = [strip(1, s) for s in range(3)]
    east0, north0 = east_hi + east_lo, north_hi + north_lo
    cos0, sin0, cos1, sin1 = [misc[r : r + 1] for r in range(4)]
    lane1 = iota((1, LANES), 1)
    edge_of = lane_pick(lane1 >> 5, edges)

    far_e, far_n, far_qe, far_qn, far_c, far_cos, far_sin = (zero,) * 7
    own_qe, own_qn, last_e, last_n = (zero,) * 4
    side_v = jnp.zeros((1, LANES), jnp.int32)
    far_edge_v, far_side_v = side_v, side_v

    def code_at(top, e):
        codes = top * 8.0 + roll(top, -4)
        return jnp.sum(jnp.where((level == 4) & (lane == 96 + e), codes, 0.0)).astype(jnp.int32)

    for e in range(4):
        for end in range(2):
            here = lane == 32 * e + 31 * end
            here1 = lane1 == 32 * e + 31 * end
            goal = 32 * e + 31 * end + LANES

            def take(into, vector, source):
                return jnp.where(here, pltpu.roll(vector, (goal - source) & 127, 1), into)

            even = (edges[e] & 1) == 0
            side = jnp.where(even, 1 if end else 3, 0 if end else 2)
            high = (edges[e] < 2).astype(jnp.int32)
            c2 = corner_of(edges[e], end)
            q2 = jnp.where(even, 2, 1)
            own_qe = take(own_qe, near[e][1], 96 + 4 * c2 + q2)
            own_qn = take(own_qn, near[e][1], 112 + 4 * c2 + q2)
            code = code_at(near[e][0], side)
            far_edge, far_flip = (code >> 1) & 3, code & 1
            far_top, far_low = packet(jnp.clip(code >> 3, 0, TILES - 1))
            end3 = high ^ far_flip
            c3 = corner_of(far_edge, end3)
            q3 = jnp.where((far_edge & 1) == 0, 1, 2)
            far_e = take(far_e, far_low, 96 + 4 * c3)
            far_n = take(far_n, far_low, 112 + 4 * c3)
            far_qe = take(far_qe, far_low, 96 + 4 * c3 + q3)
            far_qn = take(far_qn, far_low, 112 + 4 * c3 + q3)
            far_c = take(far_c, far_low, 96 + 4 * c3 + 3)
            far_trig = take(zero, far_top, 96 + 4 * c3)
            far_cos, far_sin = far_cos + far_trig[6:7], far_sin + far_trig[5:6]
            far_side = jnp.where(
                (far_edge & 1) == 0, jnp.where(end3 == 1, 1, 3), jnp.where(end3 == 1, 0, 2)
            )
            code = code_at(far_top, far_side)
            last_edge, last_flip = (code >> 1) & 3, code & 1
            _, last_low = packet(jnp.clip(code >> 3, 0, TILES - 1))
            c4 = corner_of(last_edge, (far_edge < 2).astype(jnp.int32) ^ last_flip)
            last_e = take(last_e, last_low, 96 + 4 * c4)
            last_n = take(last_n, last_low, 112 + 4 * c4)
            side_v = jnp.where(here1, side, side_v)
            far_edge_v = jnp.where(here1, far_edge, far_edge_v)
            far_side_v = jnp.where(here1, far_side, far_side_v)

    place = place_ref[...]
    cell = iota((1, CELLS), 1)
    row, col = cell >> 5, cell & (TS - 1)
    along_x = (group & 1) == 1

    def rims_of(fields):
        hi, lo = halves(fields)
        got = dot(jnp.concatenate([hi, lo], axis=0).astype(BF16), place, ((1,), (1,)))
        return got[: fields.shape[0]] + got[fields.shape[0] :]

    def placed(pairs):
        parts = [p for pair in pairs for p in pair]
        parts = [jnp.where(along_x, p, 0.0) for p in parts] + [jnp.where(along_x, 0.0, p) for p in parts]
        got = dot(jnp.concatenate(parts, axis=0).astype(BF16), place)
        got = [got[LEV * i : LEV * (i + 1)] for i in range(len(parts))]
        got = [got[i] + got[i + 1] for i in range(0, len(got), 2)]
        return [(got[i], got[i + len(pairs)]) for i in range(len(pairs))]

    def shifts(h, halo):
        halo_x, halo_y = halo
        return (
            jnp.where(col == TS - 1, halo_x, roll(h, -1)),
            jnp.where(col == 0, halo_x, roll(h, 1)),
            jnp.where(row == TS - 1, halo_y, roll(h, -TS)),
            jnp.where(row == 0, halo_y, roll(h, TS)),
        )

    wind = wind_ref[...]
    east, north = wind[:LEV], wind[LEV:]
    cosine, sine = trig_ref[0:1, :], trig_ref[1:2, :]
    rim = rims_of(wind)
    rim_e, rim_n = rim[:LEV], rim[LEV:]
    halo_e, halo_n = placed([(east_hi, east_lo), (north_hi, north_lo)])
    ex, exm, ey, eym = shifts(east, halo_e)
    nx, nxm, ny, nym = shifts(north, halo_n)
    along = cosine * (0.5 * (east + ey)) + sine * (0.5 * (north + ny))
    across = -sine * (0.5 * (east + ex)) + cosine * (0.5 * (north + nx))
    dgrid_ref[...] = jnp.concatenate([along, across], axis=0).astype(BF16)
    vortex = cosine * (0.5 * (nx - nxm) - 0.5 * (ey - eym)) - sine * (0.5 * (ex - exm) + 0.5 * (ny - nym))

    c0 = c0 + towards(edge_of, cos0, sin0, rim_e - east0, rim_n - north0)
    ends = (at == 0) | (at == 31)
    c0 = c0 + jnp.where(ends, towards(side_v, cos0, sin0, far_e - east0, far_n - north0), 0.0)
    c1 = c1 + jnp.where(ends, towards(side_v, cos1, sin1, far_qe - own_qe, far_qn - own_qn), 0.0)
    far_c = far_c + towards(far_edge_v, far_cos, far_sin, east0 - far_e, north0 - far_n)
    far_c = far_c + towards(far_side_v, far_cos, far_sin, last_e - far_e, last_n - far_n)

    rim_c = rims_of(vortex)
    after = jnp.where(at == 31, far_c, roll(c0, -1))
    before = jnp.where(at == 0, far_c, roll(c0, 1))
    s0 = c0 + 0.2 * (c1 + rim_c + after + before - 4.0 * c0)
    halo_c, halo_s = placed([halves(c0), halves(s0)])
    for halo in (halo_c, halo_s):
        xp, xm, yp, ym = shifts(vortex, halo)
        vortex = vortex + 0.2 * (xp + xm + yp + ym - 4.0 * vortex)
    vortex_ref[...] = vortex


def vmem():
    return pl.BlockSpec(memory_space=pltpu.VMEM)


def smem():
    return pl.BlockSpec(memory_space=pltpu.SMEM)


def shape(dims, kind):
    return jax.ShapeDtypeStruct(dims, kind)


def anywhere():
    return pl.BlockSpec(memory_space=pl.ANY)


def hbm():
    return pl.BlockSpec(memory_space=pltpu.HBM)


def cost(flops, moved):
    return pl.CostEstimate(flops=flops, bytes_accessed=moved, transcendentals=0)


def body(checkpoint, remap_weights, margins, seams, rotation_angle):
    own_margins = margins[0, 0]
    weights = remap_weights[0, 0].reshape(K * SB, CELLS)
    limit = pltpu.CompilerParams(vmem_limit_bytes=16 * MIB)

    asked = pl.pallas_call(
        ask_kernel,
        out_shape=shape((N_TILE, 1, LANES), jnp.int32),
        in_specs=[hbm()],
        out_specs=vmem(),
        scratch_shapes=[pltpu.SMEM((K,), jnp.int32), pltpu.SemaphoreType.DMA],
        name="ask",
    )(own_margins)
    asked = lax.all_to_all(asked, "tile", 0, 0, tiled=True).reshape(N_TILE, LANES)

    meta, held = pl.pallas_call(
        prepare_kernel,
        out_shape=(shape((LEV, LANES), jnp.int32), shape(checkpoint.shape, BF16)),
        in_specs=[smem(), smem(), hbm()],
        out_specs=(vmem(),) * 2,
        scratch_shapes=[pltpu.SemaphoreType.DMA],
        compiler_params=limit,
        cost_estimate=cost(1 << 20, MIB),
        name="prepare",
    )(own_margins, seams[0, 0], checkpoint)
    blocks = pl.pallas_call(
        select_kernel,
        out_shape=shape((N_TILE, ROWS, CAP * SB), BF16),
        in_specs=[smem(), vmem()],
        out_specs=anywhere(),
        scratch_shapes=[pltpu.SemaphoreType.DMA((N_TILE, CAP))],
        compiler_params=limit,
        name="select",
    )(asked, held)
    blocks = lax.all_to_all(blocks, "tile", 0, 0, tiled=True)

    weights = pltpu.with_memory_space_constraint(weights, pltpu.HBM)
    head = pl.pallas_call(
        fetch_kernel,
        out_shape=shape((HEAD, CELLS), BF16),
        in_specs=[hbm(), anywhere()],
        out_specs=vmem(),
        scratch_shapes=[pltpu.SemaphoreType.DMA],
        compiler_params=limit,
        cost_estimate=cost(1 << 20, 4 * MIB),
        name="fetch",
    )(weights, asked)

    scalars, wind, trig, place, packets = pl.pallas_call(
        remap_kernel,
        out_shape=(
            shape((ROWS - WINDS, CELLS), BF16),
            shape((WINDS, CELLS), F32),
            shape((LEV, CELLS), F32),
            shape((LANES, CELLS), BF16),
            shape((TILES, 16, LANES), BF16),
        ),
        in_specs=[smem(), vmem(), vmem(), hbm(), vmem()],
        out_specs=(anywhere(),) + (vmem(),) * 4,
        scratch_shapes=[
            pltpu.VMEM((ROWS, K * SB), BF16),
            pltpu.VMEM((K * SB - HEAD, CELLS), BF16),
            pltpu.VMEM((CELLS, 3 * LANES), BF16),
            pltpu.VMEM((ROWS - WINDS, CELLS), BF16),
            pltpu.SemaphoreType.DMA(((K * SB - HEAD) // CHUNK,)),
            pltpu.SemaphoreType.DMA,
        ],
        compiler_params=limit,
        cost_estimate=cost(2 * ROWS * K * SB * CELLS, 9 * MIB),
        name="remap",
    )(meta, blocks, head, weights, rotation_angle[0, 0].reshape(1, CELLS))
    packets = lax.all_to_all(packets, ("face", "tile"), 0, 0, tiled=True)

    dgrid, vortex = pl.pallas_call(
        smooth_kernel,
        out_shape=(shape((WINDS, CELLS), BF16), shape((LEV, CELLS), F32)),
        in_specs=[smem()] + [vmem()] * 4,
        out_specs=(vmem(), vmem()),
        compiler_params=limit,
        name="smooth",
    )(meta, packets, wind, trig, place)
    return (
        scalars.reshape(1, 1, ROWS - WINDS, CELLS),
        dgrid.reshape(1, 1, WINDS, CELLS),
        vortex.reshape(1, 1, LEV, CELLS),
    )


def solution(mesh):
    placed = (
        P(None, "tile"),
        P("face", "tile", None, None, None),
        P("face", "tile", None),
        P("face", "tile", None, None),
        P("face", "tile", None),
    )
    return jax.shard_map(
        body,
        mesh=mesh,
        in_specs=placed,
        out_specs=(P("face", "tile", None, None),) * 3,
        check_vma=False,
    )
```

```python
import jax
import jax.numpy as jnp
from jax import lax
from jax.experimental import pallas as pl
from jax.experimental.pallas import tpu as pltpu
from jax.sharding import PartitionSpec as P

LEV = 8
FIELDS = 6
TS = 32
CELLS = TS * TS
SB = 256
BLK_DEV = 8
K = 16
CAP = 2
GROUPS = K // CAP
N_TILE = 16
TILES = 128
ROWS = FIELDS * LEV
WINDS = 2 * LEV
LANES = 128
MIB = 1 << 20
HEAD = 1024
CHUNK = 256
PARTS = 4
F32 = jnp.float32
BF16 = jnp.bfloat16


def iota(shape, dim):
    return lax.broadcasted_iota(jnp.int32, shape, dim)


def dot(a, b, contract=((1,), (0,))):
    return lax.dot_general(a, b, (contract, ((), ())), preferred_element_type=F32)


def halves(x):
    hi = x.astype(BF16).astype(F32)
    return hi, x - hi


def roll(x, shift):
    return pltpu.roll(x, shift % x.shape[1], 1)


def lane_pick(group, values):
    out = jnp.full(group.shape, values[0])
    for index in range(1, len(values)):
        out = jnp.where(group == index, values[index], out)
    return out


def towards(direction, cosine, sine, d_east, d_north):
    a_east = jnp.where(
        direction == 0, -cosine, jnp.where(direction == 1, -sine, jnp.where(direction == 2, cosine, sine))
    )
    a_north = jnp.where(
        direction == 0, -sine, jnp.where(direction == 1, cosine, jnp.where(direction == 2, sine, -cosine))
    )
    return 0.5 * (a_east * d_east + a_north * d_north)


def neighbours_within(h, row, col):
    return (
        jnp.where(col == TS - 1, h, roll(h, -1)),
        jnp.where(col == 0, h, roll(h, 1)),
        jnp.where(row == TS - 1, h, roll(h, -TS)),
        jnp.where(row == 0, h, roll(h, TS)),
    )


def ask_kernel(margins_ref, checkpoint_ref, asked_ref, held_ref, margins, sems):
    copies = [
        pltpu.make_async_copy(margins_ref, margins, sems.at[0]),
        pltpu.make_async_copy(checkpoint_ref, held_ref, sems.at[1]),
    ]
    for copy in copies:
        copy.start()
    copies[0].wait()
    reader, lane = iota((N_TILE, LANES), 0), iota((N_TILE, LANES), 1)
    asked = jnp.zeros((N_TILE, LANES), jnp.int32)
    for m in range(GROUPS):
        first, second = margins[CAP * m], margins[CAP * m + 1]
        asked = jnp.where(reader == (first >> 3), jnp.where(lane == 0, first, second), asked)
    asked = asked & (BLK_DEV - 1)
    for r in range(N_TILE):
        asked_ref[r] = asked[r : r + 1]
    copies[1].wait()


def select_kernel(asked_ref, held_ref, out_ref, staged, sems):
    copies = []
    for part in range(PARTS):
        span = N_TILE // PARTS
        for g in range(part * span, (part + 1) * span):
            for j in range(CAP):
                block = asked_ref[g, j] & (BLK_DEV - 1)
                staged[g, :, j * SB : (j + 1) * SB] = held_ref[:, pl.ds(pl.multiple_of(block * SB, SB), SB)]
        where = pl.ds(part * span, span)
        copies.append(pltpu.make_async_copy(staged.at[where], out_ref.at[where], sems.at[part]))
        copies[-1].start()
    for copy in copies:
        copy.wait()


def fetch_kernel(margins_ref, seams_ref, weights_ref, head_ref, meta_ref, sem):
    copy = pltpu.make_async_copy(weights_ref.at[pl.ds(0, HEAD)], head_ref, sem)
    copy.start()
    level, lane = iota((LEV, LANES), 0), iota((LEV, LANES), 1)
    meta = jnp.zeros((LEV, LANES), jnp.int32)
    for m in range(GROUPS):
        reader = jnp.clip(margins_ref[CAP * m] >> 3, 0, N_TILE - 1)
        meta = jnp.where((level == 0) & (lane == m), reader, meta)
    for kind in range(3):
        for e in range(4):
            meta = jnp.where((level == kind + 1) & (lane == e), seams_ref[kind, 0, e], meta)
    meta_ref[...] = meta
    copy.wait()


def remap_kernel(
    meta_ref, blocks_ref, head_ref, weights_ref, angle_ref,
    scalars_ref, wind_ref, trig_ref, place_ref, send_ref,
    chosen, streamed, pick_ref, sems,
):
    spans = [(k, pl.ds(k, CHUNK)) for k in range(HEAD, K * SB, CHUNK)]
    copies = [
        pltpu.make_async_copy(weights_ref.at[span], streamed.at[pl.ds(k - HEAD, CHUNK)], sems.at[index])
        for index, (k, span) in enumerate(spans)
    ]
    for copy in copies:
        copy.start()
    for m in range(GROUPS):
        chosen[:, CAP * SB * m : CAP * SB * (m + 1)] = blocks_ref[meta_ref[0, m]]
    total = dot(chosen[:, :HEAD], head_ref[...])

    angle = angle_ref[...]
    trig_ref[...] = jnp.where((iota((LEV, CELLS), 0) & 1) == 0, jnp.cos(angle), jnp.sin(angle))

    lane = iota((1, 3 * LANES), 1)
    edge, depth, at = (lane >> 6) & 3, (lane >> 5) & 1, lane & 31
    rim_cell = jnp.where(
        edge == 0, (TS - 1 - depth) * TS + at,
        jnp.where(edge == 1, at * TS + TS - 1 - depth, jnp.where(edge == 2, depth * TS + at, at * TS + depth)),
    )
    corner, k = (lane >> 2) & 3, lane & 3
    c_row, c_col = (corner >> 1) * (TS - 1), (corner & 1) * (TS - 1)
    c_row = jnp.where(k == 2, jnp.where(c_row == 0, 1, TS - 2), c_row)
    c_col = jnp.where(k == 1, jnp.where(c_col == 0, 1, TS - 2), c_col)
    corner_cell = jnp.where((lane & 127) >= 96, c_row * TS + c_col, -1)
    taken = jnp.where(lane < 2 * LANES, rim_cell, corner_cell)
    pick_ref[...] = (iota((CELLS, 3 * LANES), 0) == taken).astype(F32).astype(BF16)

    line = iota((LANES, 1), 0)
    line_edge, line_at = line >> 5, line & 31
    flipped = lane_pick(line_edge, [meta_ref[3, e] for e in range(4)]) == 1
    line_at = jnp.where(flipped, TS - 1 - line_at, line_at)
    rim_cell = jnp.where(
        line_edge == 0, (TS - 1) * TS + line_at,
        jnp.where(line_edge == 1, line_at * TS + TS - 1, jnp.where(line_edge == 2, line_at, line_at * TS)),
    )
    place_ref[...] = (iota((LANES, CELLS), 1) == rim_cell).astype(F32).astype(BF16)

    for copy, (k, _) in zip(copies, spans):
        copy.wait()
        total = total + dot(chosen[:, k : k + CHUNK], streamed[k - HEAD : k - HEAD + CHUNK])
    scalars_ref[...] = total[WINDS:].astype(BF16)
    wind = total[:WINDS]
    wind_ref[...] = wind
    east, north = wind[:LEV], wind[LEV:]

    cell = iota((1, CELLS), 1)
    row, col = cell >> 5, cell & (TS - 1)
    trig = trig_ref[...]
    cosine, sine = trig[0:1], trig[1:2]
    ex, exm, ey, eym = neighbours_within(east, row, col)
    nx, nxm, ny, nym = neighbours_within(north, row, col)
    curl = cosine * (0.5 * (nx - nxm) - 0.5 * (ey - eym)) - sine * (0.5 * (ex - exm) + 0.5 * (ny - nym))

    hi, lo = halves(jnp.concatenate([east, north, curl, trig], axis=0))
    got = dot(jnp.concatenate([hi, lo], axis=0).astype(BF16), pick_ref[...])

    lane = iota((LEV, LANES), 1)
    level = iota((LEV, LANES), 0)
    group = lane >> 5
    corners = got[:, 2 * LANES :]
    common_top = jnp.where((level == 5) | (level == 6), corners[24:32], 0.0)
    for e in range(4):
        tile = meta_ref[1, e].astype(F32)
        code = (meta_ref[2, e] * 2 + meta_ref[3, e]).astype(F32)
        common_top = jnp.where((level == 4) & (lane == 96 + e), tile, common_top)
        common_top = jnp.where((level == 4) & (lane == 100 + e), code, common_top)
    common_low = jnp.where(
        lane >= 112, corners[8:16], jnp.where((lane & 3) == 3, corners[16:24], corners[0:8])
    )
    common_low = jnp.where(group == 3, common_low, 0.0)
    common = jnp.concatenate([common_top, common_low], axis=0).astype(BF16)
    for t in range(TILES):
        send_ref[t] = common
    for e in range(4):
        rim = roll(got[:, LANES * (e // 2) : LANES * (e // 2 + 1)], -64 * (e % 2))
        top = jnp.where(
            group == 0, rim[0:8],
            jnp.where(group == 1, roll(rim[32:40], 32), jnp.where(group == 2, roll(rim[16:24], 64), common_top)),
        )
        top = jnp.where((group == 3) & (level < 2), roll(rim[24:32], 96), top)
        top = jnp.where((group == 3) & ((level == 2) | (level == 3)), roll(rim[24:32], 64), top)
        low = jnp.where(
            group == 0, rim[8:16],
            jnp.where(group == 1, roll(rim[40:48], 32), jnp.where(group == 2, roll(rim[16:24], 32), common_low)),
        )
        send_ref[jnp.clip(meta_ref[1, e], 0, TILES - 1)] = jnp.concatenate([top, low], axis=0).astype(BF16)


def smooth_kernel(
    meta_ref, packets_ref, wind_ref, trig_ref, place_ref, scalars_ref, scalars_out_ref, dgrid_ref, vortex_ref
):
    def packet(tile):
        both = packets_ref[tile].astype(F32)
        return both[:LEV], both[LEV:]

    def corner_of(edge, end):
        return jnp.where((edge & 1) == 0, jnp.where(edge == 0, 2, 0) + end, 2 * end + jnp.where(edge == 1, 1, 0))

    scalars_out_ref[...] = scalars_ref[...]
    lane = iota((LEV, LANES), 1)
    group = lane >> 5
    at = lane & 31
    zero = jnp.zeros((LEV, LANES), F32)
    edges = [meta_ref[2, e] for e in range(4)]
    near = [packet(jnp.clip(meta_ref[1, e], 0, TILES - 1)) for e in range(4)]

    def code_of(top, edge):
        codes = pltpu.roll(top * 8.0 + roll(top, -4), (LANES - 96 - edge) & 127, 1)
        return codes[4, 0].astype(jnp.int32)

    def strip(half, source):
        out = roll(near[0][half], -32 * source)
        for e in range(1, 4):
            out = jnp.where(group == e, roll(near[e][half], 32 * (e - source)), out)
        return out

    east_hi, east_lo, c0, misc = [strip(0, s) for s in range(4)]
    north_hi, north_lo, c1 = [strip(1, s) for s in range(3)]
    east0, north0 = east_hi + east_lo, north_hi + north_lo
    cos0, sin0, cos1, sin1 = [misc[r : r + 1] for r in range(4)]
    lane1 = iota((1, LANES), 1)
    edge_of = lane_pick(lane1 >> 5, edges)

    spots = [(e, end) for e in range(4) for end in range(2)]

    def take(into, vector, source, spot):
        goal = 32 * spot[0] + 31 * spot[1]
        return jnp.where(lane == goal, pltpu.roll(vector, (goal + LANES - source) & 127, 1), into)

    def mark(into, value, spot):
        return jnp.where(lane1 == 32 * spot[0] + 31 * spot[1], value, into)

    own_qe, own_qn = zero, zero
    side_v = jnp.zeros((1, LANES), jnp.int32)
    sides = []
    for spot in spots:
        e, end = spot
        even = (edges[e] & 1) == 0
        side = jnp.where(even, 1 if end else 3, 0 if end else 2)
        corner = corner_of(edges[e], end)
        beside = jnp.where(even, 2, 1)
        own_qe = take(own_qe, near[e][1], 96 + 4 * corner + beside, spot)
        own_qn = take(own_qn, near[e][1], 112 + 4 * corner + beside, spot)
        side_v = mark(side_v, side, spot)
        sides.append(side)

    far = []
    for spot, side in zip(spots, sides):
        code = code_of(near[spot[0]][0], side)
        end = (edges[spot[0]] < 2).astype(jnp.int32) ^ (code & 1)
        far.append((packet(jnp.clip(code >> 3, 0, TILES - 1)), (code >> 1) & 3, end))

    far_e, far_n, far_qe, far_qn, far_c, far_cos, far_sin = (zero,) * 7
    far_edge_v, far_side_v = jnp.zeros_like(side_v), jnp.zeros_like(side_v)
    sides = []
    for spot, ((top, low), edge, end) in zip(spots, far):
        corner = corner_of(edge, end)
        even = (edge & 1) == 0
        beside = jnp.where(even, 1, 2)
        side = jnp.where(even, jnp.where(end == 1, 1, 3), jnp.where(end == 1, 0, 2))
        far_e = take(far_e, low, 96 + 4 * corner, spot)
        far_n = take(far_n, low, 112 + 4 * corner, spot)
        far_qe = take(far_qe, low, 96 + 4 * corner + beside, spot)
        far_qn = take(far_qn, low, 112 + 4 * corner + beside, spot)
        far_c = take(far_c, low, 96 + 4 * corner + 3, spot)
        trig = take(zero, top, 96 + 4 * corner, spot)
        far_cos, far_sin = far_cos + trig[6:7], far_sin + trig[5:6]
        far_edge_v = mark(far_edge_v, edge, spot)
        far_side_v = mark(far_side_v, side, spot)
        sides.append(side)

    place = place_ref[...]
    cell = iota((1, CELLS), 1)
    row, col = cell >> 5, cell & (TS - 1)
    along_x = (group & 1) == 1

    def rims_of(fields):
        hi, lo = halves(fields)
        got = dot(jnp.concatenate([hi, lo], axis=0).astype(BF16), place, ((1,), (1,)))
        return got[: fields.shape[0]] + got[fields.shape[0] :]

    def placed(pairs):
        parts = [p for pair in pairs for p in pair]
        parts = [jnp.where(along_x, p, 0.0) for p in parts] + [jnp.where(along_x, 0.0, p) for p in parts]
        got = dot(jnp.concatenate(parts, axis=0).astype(BF16), place)
        got = [got[LEV * i : LEV * (i + 1)] for i in range(len(parts))]
        got = [got[i] + got[i + 1] for i in range(0, len(got), 2)]
        return [(got[i], got[i + len(pairs)]) for i in range(len(pairs))]

    def shifts(h, halo):
        halo_x, halo_y = halo
        return (
            jnp.where(col == TS - 1, halo_x, roll(h, -1)),
            jnp.where(col == 0, halo_x, roll(h, 1)),
            jnp.where(row == TS - 1, halo_y, roll(h, -TS)),
            jnp.where(row == 0, halo_y, roll(h, TS)),
        )

    wind = wind_ref[...]
    east, north = wind[:LEV], wind[LEV:]
    cosine, sine = trig_ref[0:1, :], trig_ref[1:2, :]
    rim = rims_of(wind)
    rim_e, rim_n = rim[:LEV], rim[LEV:]

    c0 = c0 + towards(edge_of, cos0, sin0, rim_e - east0, rim_n - north0)
    ends = (at == 0) | (at == 31)
    c0 = c0 + jnp.where(ends, towards(side_v, cos0, sin0, far_e - east0, far_n - north0), 0.0)
    c1 = c1 + jnp.where(ends, towards(side_v, cos1, sin1, far_qe - own_qe, far_qn - own_qn), 0.0)
    far_c = far_c + towards(far_edge_v, far_cos, far_sin, east0 - far_e, north0 - far_n)

    last_e, last_n = zero, zero
    for index, (spot, side) in enumerate(zip(spots, sides)):
        code = code_of(far[index][0][0], side)
        end = (far[index][1] < 2).astype(jnp.int32) ^ (code & 1)
        corner = corner_of((code >> 1) & 3, end)
        _, low = packet(jnp.clip(code >> 3, 0, TILES - 1))
        last_e = take(last_e, low, 96 + 4 * corner, spot)
        last_n = take(last_n, low, 112 + 4 * corner, spot)
    far_c = far_c + towards(far_side_v, far_cos, far_sin, last_e - far_e, last_n - far_n)
    after = jnp.where(at == 31, far_c, roll(c0, -1))
    before = jnp.where(at == 0, far_c, roll(c0, 1))
    s0 = c0 + 0.2 * (c1 + after + before - 4.0 * c0)
    halo_e, halo_n, halo_c, halo_s = placed(
        [(east_hi, east_lo), (north_hi, north_lo), halves(c0), halves(s0)]
    )

    ex, exm, ey, eym = shifts(east, halo_e)
    nx, nxm, ny, nym = shifts(north, halo_n)
    along = cosine * (0.5 * (east + ey)) + sine * (0.5 * (north + ny))
    across = -sine * (0.5 * (east + ex)) + cosine * (0.5 * (north + nx))
    dgrid_ref[...] = jnp.concatenate([along, across], axis=0).astype(BF16)
    vortex = cosine * (0.5 * (nx - nxm) - 0.5 * (ey - eym)) - sine * (0.5 * (ex - exm) + 0.5 * (ny - nym))
    halo_s = tuple(h + 0.2 * vortex for h in halo_s)
    for halo in (halo_c, halo_s):
        xp, xm, yp, ym = shifts(vortex, halo)
        vortex = vortex + 0.2 * (xp + xm + yp + ym - 4.0 * vortex)
    vortex_ref[...] = vortex


def vmem():
    return pl.BlockSpec(memory_space=pltpu.VMEM)


def smem():
    return pl.BlockSpec(memory_space=pltpu.SMEM)


def shape(dims, kind):
    return jax.ShapeDtypeStruct(dims, kind)


def anywhere():
    return pl.BlockSpec(memory_space=pl.ANY)


def hbm():
    return pl.BlockSpec(memory_space=pltpu.HBM)


def cost(flops, moved):
    return pl.CostEstimate(flops=flops, bytes_accessed=moved, transcendentals=0)


def body(checkpoint, remap_weights, margins, seams, rotation_angle):
    own_margins = margins[0, 0]
    weights = remap_weights[0, 0].reshape(K * SB, CELLS)
    limit = pltpu.CompilerParams(vmem_limit_bytes=16 * MIB)

    def in_hbm(x):
        return pltpu.with_memory_space_constraint(x, pltpu.HBM)

    asked, held = pl.pallas_call(
        ask_kernel,
        out_shape=(shape((N_TILE, 1, LANES), jnp.int32), shape(checkpoint.shape, BF16)),
        in_specs=[hbm(), hbm()],
        out_specs=(vmem(),) * 2,
        scratch_shapes=[pltpu.SMEM((K,), jnp.int32), pltpu.SemaphoreType.DMA((2,))],
        compiler_params=limit,
        name="ask",
    )(in_hbm(own_margins), in_hbm(checkpoint))
    asked = lax.all_to_all(asked, "tile", 0, 0, tiled=True).reshape(N_TILE, LANES)
    asked, own_margins, own_seams, angle = lax.optimization_barrier(
        (asked, own_margins, seams.reshape(3, 1, 4), rotation_angle[0, 0].reshape(1, CELLS))
    )

    blocks = pl.pallas_call(
        select_kernel,
        out_shape=shape((N_TILE, ROWS, CAP * SB), BF16),
        in_specs=[smem(), vmem()],
        out_specs=anywhere(),
        scratch_shapes=[pltpu.VMEM((N_TILE, ROWS, CAP * SB), BF16), pltpu.SemaphoreType.DMA((PARTS,))],
        compiler_params=limit,
        name="select",
    )(asked, held)
    blocks = lax.all_to_all(blocks, "tile", 0, 0, tiled=True)

    weights = in_hbm(weights)
    head, meta = pl.pallas_call(
        fetch_kernel,
        out_shape=(shape((HEAD, CELLS), BF16), shape((LEV, LANES), jnp.int32)),
        in_specs=[smem(), smem(), hbm()],
        out_specs=(vmem(),) * 2,
        scratch_shapes=[pltpu.SemaphoreType.DMA],
        compiler_params=limit,
        cost_estimate=cost(1 << 20, 4 * MIB),
        name="fetch",
    )(own_margins, own_seams, weights)

    scalars, wind, trig, place, packets = pl.pallas_call(
        remap_kernel,
        out_shape=(
            shape((ROWS - WINDS, CELLS), BF16),
            shape((WINDS, CELLS), F32),
            shape((LEV, CELLS), F32),
            shape((LANES, CELLS), BF16),
            shape((TILES, 16, LANES), BF16),
        ),
        in_specs=[smem(), vmem(), vmem(), hbm(), vmem()],
        out_specs=(vmem(),) * 5,
        scratch_shapes=[
            pltpu.VMEM((ROWS, K * SB), BF16),
            pltpu.VMEM((K * SB - HEAD, CELLS), BF16),
            pltpu.VMEM((CELLS, 3 * LANES), BF16),
            pltpu.SemaphoreType.DMA(((K * SB - HEAD) // CHUNK,)),
        ],
        compiler_params=limit,
        cost_estimate=cost(2 * ROWS * K * SB * CELLS, 9 * MIB),
        name="remap",
    )(meta, blocks, head, weights, angle)
    packets = lax.all_to_all(packets, ("face", "tile"), 0, 0, tiled=True)

    scalars, dgrid, vortex = pl.pallas_call(
        smooth_kernel,
        out_shape=(
            shape((ROWS - WINDS, CELLS), BF16),
            shape((WINDS, CELLS), BF16),
            shape((LEV, CELLS), F32),
        ),
        in_specs=[smem()] + [vmem()] * 5,
        out_specs=(vmem(),) * 3,
        compiler_params=limit,
        name="smooth",
    )(meta, packets, wind, trig, place, scalars)
    return (
        scalars.reshape(1, 1, ROWS - WINDS, CELLS),
        dgrid.reshape(1, 1, WINDS, CELLS),
        vortex.reshape(1, 1, LEV, CELLS),
    )


def solution(mesh):
    placed = (
        P(None, "tile"),
        P("face", "tile", None, None, None),
        P("face", "tile", None),
        P("face", "tile", None, None),
        P("face", "tile", None),
    )
    return jax.shard_map(
        body,
        mesh=mesh,
        in_specs=placed,
        out_specs=(P("face", "tile", None, None),) * 3,
        check_vma=False,
    )
```

```python
import jax
import jax.numpy as jnp
from jax import lax
from jax.experimental import pallas as pl
from jax.experimental.pallas import tpu as pltpu
from jax.sharding import PartitionSpec as P

LEV = 8
FIELDS = 6
TS = 32
CELLS = TS * TS
SB = 256
BLK_DEV = 8
K = 16
CAP = 2
GROUPS = K // CAP
N_TILE = 16
TILES = 128
ROWS = FIELDS * LEV
WINDS = 2 * LEV
LANES = 128
MIB = 1 << 20
CHUNK = 256
F32 = jnp.float32
BF16 = jnp.bfloat16


def iota(shape, dim):
    return lax.broadcasted_iota(jnp.int32, shape, dim)


def dot(a, b, contract=((1,), (0,))):
    return lax.dot_general(a, b, (contract, ((), ())), preferred_element_type=F32)


def halves(x):
    hi = x.astype(BF16).astype(F32)
    return hi, x - hi


def roll(x, shift):
    return pltpu.roll(x, shift % x.shape[1], 1)


def lane_pick(group, values):
    out = jnp.full(group.shape, values[0])
    for index in range(1, len(values)):
        out = jnp.where(group == index, values[index], out)
    return out


def towards(direction, cosine, sine, d_east, d_north):
    a_east = jnp.where(
        direction == 0, -cosine, jnp.where(direction == 1, -sine, jnp.where(direction == 2, cosine, sine))
    )
    a_north = jnp.where(
        direction == 0, -sine, jnp.where(direction == 1, cosine, jnp.where(direction == 2, sine, -cosine))
    )
    return 0.5 * (a_east * d_east + a_north * d_north)


def neighbours_within(h, row, col):
    return (
        jnp.where(col == TS - 1, h, roll(h, -1)),
        jnp.where(col == 0, h, roll(h, 1)),
        jnp.where(row == TS - 1, h, roll(h, -TS)),
        jnp.where(row == 0, h, roll(h, TS)),
    )


def ask_kernel(
    margins_ref, seams_ref, checkpoint_ref, asked_ref, meta_ref, held_ref, margins, seams, sems
):
    copies = [
        pltpu.make_async_copy(margins_ref, margins, sems.at[0]),
        pltpu.make_async_copy(seams_ref, seams, sems.at[1]),
        pltpu.make_async_copy(checkpoint_ref, held_ref, sems.at[2]),
    ]
    for copy in copies:
        copy.start()
    copies[0].wait()
    reader, lane = iota((N_TILE, LANES), 0), iota((N_TILE, LANES), 1)
    asked = jnp.zeros((N_TILE, LANES), jnp.int32)
    for m in range(GROUPS):
        first, second = margins[CAP * m], margins[CAP * m + 1]
        asked = jnp.where(reader == (first >> 3), jnp.where(lane == 0, first, second), asked)
    asked = asked & (BLK_DEV - 1)
    for r in range(N_TILE):
        asked_ref[r] = asked[r : r + 1]

    copies[1].wait()
    level, lane = iota((LEV, LANES), 0), iota((LEV, LANES), 1)
    meta = jnp.zeros((LEV, LANES), jnp.int32)
    for m in range(GROUPS):
        reader = jnp.clip(margins[CAP * m] >> 3, 0, N_TILE - 1)
        meta = jnp.where((level == 0) & (lane == m), reader, meta)
    for kind in range(3):
        for e in range(4):
            meta = jnp.where((level == kind + 1) & (lane == e), seams[kind, 0, e], meta)
    meta_ref[...] = meta
    copies[2].wait()


def slot(tile):
    tile = jnp.clip(tile, 0, TILES - 1)
    return (tile & (N_TILE - 1)) * (TILES // N_TILE) + (tile >> 4)


def select_kernel(asked_ref, held_ref, out_ref):
    for g in range(N_TILE):
        for j in range(CAP):
            block = asked_ref[g, j] & (BLK_DEV - 1)
            out_ref[g, :, j * SB : (j + 1) * SB] = held_ref[:, pl.ds(pl.multiple_of(block * SB, SB), SB)]


def remap_kernel(
    meta_ref, blocks_ref, weights_ref, angle_ref,
    scalars_ref, wind_ref, trig_ref, place_ref, send_ref,
    chosen, streamed, pick_ref, angle, sems,
):
    angle_copy = pltpu.make_async_copy(angle_ref, angle, sems.at[K * SB // CHUNK])
    angle_copy.start()
    spans = [(k, pl.ds(k, CHUNK)) for k in range(0, K * SB, CHUNK)]
    copies = [
        pltpu.make_async_copy(weights_ref.at[span], streamed.at[span], sems.at[index])
        for index, (k, span) in enumerate(spans)
    ]
    for copy in copies:
        copy.start()
    for m in range(GROUPS):
        chosen[:, CAP * SB * m : CAP * SB * (m + 1)] = blocks_ref[meta_ref[0, m]]
    total = None

    angle_copy.wait()
    trig_ref[...] = jnp.where((iota((LEV, CELLS), 0) & 1) == 0, jnp.cos(angle[...]), jnp.sin(angle[...]))

    lane = iota((1, 3 * LANES), 1)
    edge, depth, at = (lane >> 6) & 3, (lane >> 5) & 1, lane & 31
    rim_cell = jnp.where(
        edge == 0, (TS - 1 - depth) * TS + at,
        jnp.where(edge == 1, at * TS + TS - 1 - depth, jnp.where(edge == 2, depth * TS + at, at * TS + depth)),
    )
    corner, k = (lane >> 2) & 3, lane & 3
    c_row, c_col = (corner >> 1) * (TS - 1), (corner & 1) * (TS - 1)
    c_row = jnp.where(k == 2, jnp.where(c_row == 0, 1, TS - 2), c_row)
    c_col = jnp.where(k == 1, jnp.where(c_col == 0, 1, TS - 2), c_col)
    corner_cell = jnp.where((lane & 127) >= 96, c_row * TS + c_col, -1)
    taken = jnp.where(lane < 2 * LANES, rim_cell, corner_cell)
    pick_ref[...] = (iota((CELLS, 3 * LANES), 0) == taken).astype(F32).astype(BF16)

    line = iota((LANES, 1), 0)
    line_edge, line_at = line >> 5, line & 31
    flipped = lane_pick(line_edge, [meta_ref[3, e] for e in range(4)]) == 1
    line_at = jnp.where(flipped, TS - 1 - line_at, line_at)
    rim_cell = jnp.where(
        line_edge == 0, (TS - 1) * TS + line_at,
        jnp.where(line_edge == 1, line_at * TS + TS - 1, jnp.where(line_edge == 2, line_at, line_at * TS)),
    )
    place_ref[...] = (iota((LANES, CELLS), 1) == rim_cell).astype(F32).astype(BF16)

    for copy, (k, _) in zip(copies, spans):
        copy.wait()
        part = dot(chosen[:, k : k + CHUNK], streamed[k : k + CHUNK])
        total = part if total is None else total + part
    scalars_ref[...] = total[WINDS:].astype(BF16)
    wind = total[:WINDS]
    wind_ref[...] = wind
    east, north = wind[:LEV], wind[LEV:]

    cell = iota((1, CELLS), 1)
    row, col = cell >> 5, cell & (TS - 1)
    trig = trig_ref[...]
    cosine, sine = trig[0:1], trig[1:2]
    ex, exm, ey, eym = neighbours_within(east, row, col)
    nx, nxm, ny, nym = neighbours_within(north, row, col)
    curl = cosine * (0.5 * (nx - nxm) - 0.5 * (ey - eym)) - sine * (0.5 * (ex - exm) + 0.5 * (ny - nym))

    hi, lo = halves(jnp.concatenate([east, north, curl, trig], axis=0))
    got = dot(jnp.concatenate([hi, lo], axis=0).astype(BF16), pick_ref[...])

    lane = iota((LEV, LANES), 1)
    level = iota((LEV, LANES), 0)
    group = lane >> 5
    corners = got[:, 2 * LANES :]
    common_top = jnp.where((level == 5) | (level == 6), corners[24:32], 0.0)
    for e in range(4):
        tile = meta_ref[1, e].astype(F32)
        code = (meta_ref[2, e] * 2 + meta_ref[3, e]).astype(F32)
        common_top = jnp.where((level == 4) & (lane == 96 + e), tile, common_top)
        common_top = jnp.where((level == 4) & (lane == 100 + e), code, common_top)
    common_low = jnp.where(
        lane >= 112, corners[8:16], jnp.where((lane & 3) == 3, corners[16:24], corners[0:8])
    )
    common_low = jnp.where(group == 3, common_low, 0.0)
    common = jnp.concatenate([common_top, common_low], axis=0).astype(BF16)
    for t in range(TILES):
        send_ref[t] = common
    for e in range(4):
        rim = roll(got[:, LANES * (e // 2) : LANES * (e // 2 + 1)], -64 * (e % 2))
        top = jnp.where(
            group == 0, rim[0:8],
            jnp.where(group == 1, roll(rim[32:40], 32), jnp.where(group == 2, roll(rim[16:24], 64), common_top)),
        )
        top = jnp.where((group == 3) & (level < 2), roll(rim[24:32], 96), top)
        top = jnp.where((group == 3) & ((level == 2) | (level == 3)), roll(rim[24:32], 64), top)
        low = jnp.where(
            group == 0, rim[8:16],
            jnp.where(group == 1, roll(rim[40:48], 32), jnp.where(group == 2, roll(rim[16:24], 32), common_low)),
        )
        send_ref[slot(meta_ref[1, e])] = jnp.concatenate([top, low], axis=0).astype(BF16)


def smooth_kernel(
    meta_ref, packets_ref, wind_ref, trig_ref, place_ref, scalars_ref, scalars_out_ref, dgrid_ref, vortex_ref
):
    def packet(tile):
        both = packets_ref[slot(tile)].astype(F32)
        return both[:LEV], both[LEV:]

    def corner_of(edge, end):
        return jnp.where((edge & 1) == 0, jnp.where(edge == 0, 2, 0) + end, 2 * end + jnp.where(edge == 1, 1, 0))

    scalars_out_ref[...] = scalars_ref[...]
    lane = iota((LEV, LANES), 1)
    group = lane >> 5
    at = lane & 31
    zero = jnp.zeros((LEV, LANES), F32)
    edges = [meta_ref[2, e] for e in range(4)]
    near = [packet(meta_ref[1, e]) for e in range(4)]

    def code_of(top, edge):
        codes = pltpu.roll(top * 8.0 + roll(top, -4), (LANES - 96 - edge) & 127, 1)
        return codes[4, 0].astype(jnp.int32)

    def strip(half, source):
        out = roll(near[0][half], -32 * source)
        for e in range(1, 4):
            out = jnp.where(group == e, roll(near[e][half], 32 * (e - source)), out)
        return out

    east_hi, east_lo, c0, misc = [strip(0, s) for s in range(4)]
    north_hi, north_lo, c1 = [strip(1, s) for s in range(3)]
    east0, north0 = east_hi + east_lo, north_hi + north_lo
    cos0, sin0, cos1, sin1 = [misc[r : r + 1] for r in range(4)]
    lane1 = iota((1, LANES), 1)
    edge_of = lane_pick(lane1 >> 5, edges)

    spots = [(e, end) for e in range(4) for end in range(2)]

    def take(into, vector, source, spot):
        goal = 32 * spot[0] + 31 * spot[1]
        return jnp.where(lane == goal, pltpu.roll(vector, (goal + LANES - source) & 127, 1), into)

    def mark(into, value, spot):
        return jnp.where(lane1 == 32 * spot[0] + 31 * spot[1], value, into)

    own_qe, own_qn = zero, zero
    side_v = jnp.zeros((1, LANES), jnp.int32)
    sides = []
    for spot in spots:
        e, end = spot
        even = (edges[e] & 1) == 0
        side = jnp.where(even, 1 if end else 3, 0 if end else 2)
        corner = corner_of(edges[e], end)
        beside = jnp.where(even, 2, 1)
        own_qe = take(own_qe, near[e][1], 96 + 4 * corner + beside, spot)
        own_qn = take(own_qn, near[e][1], 112 + 4 * corner + beside, spot)
        side_v = mark(side_v, side, spot)
        sides.append(side)

    far = []
    for spot, side in zip(spots, sides):
        code = code_of(near[spot[0]][0], side)
        end = (edges[spot[0]] < 2).astype(jnp.int32) ^ (code & 1)
        far.append((packet(code >> 3), (code >> 1) & 3, end))

    far_e, far_n, far_qe, far_qn, far_c, far_cos, far_sin = (zero,) * 7
    far_edge_v, far_side_v = jnp.zeros_like(side_v), jnp.zeros_like(side_v)
    sides = []
    for spot, ((top, low), edge, end) in zip(spots, far):
        corner = corner_of(edge, end)
        even = (edge & 1) == 0
        beside = jnp.where(even, 1, 2)
        side = jnp.where(even, jnp.where(end == 1, 1, 3), jnp.where(end == 1, 0, 2))
        far_e = take(far_e, low, 96 + 4 * corner, spot)
        far_n = take(far_n, low, 112 + 4 * corner, spot)
        far_qe = take(far_qe, low, 96 + 4 * corner + beside, spot)
        far_qn = take(far_qn, low, 112 + 4 * corner + beside, spot)
        far_c = take(far_c, low, 96 + 4 * corner + 3, spot)
        trig = take(zero, top, 96 + 4 * corner, spot)
        far_cos, far_sin = far_cos + trig[6:7], far_sin + trig[5:6]
        far_edge_v = mark(far_edge_v, edge, spot)
        far_side_v = mark(far_side_v, side, spot)
        sides.append(side)

    place = place_ref[...]
    cell = iota((1, CELLS), 1)
    row, col = cell >> 5, cell & (TS - 1)
    along_x = (group & 1) == 1

    def rims_of(fields):
        hi, lo = halves(fields)
        got = dot(jnp.concatenate([hi, lo], axis=0).astype(BF16), place, ((1,), (1,)))
        return got[: fields.shape[0]] + got[fields.shape[0] :]

    def placed(pairs):
        parts = [p for pair in pairs for p in pair]
        parts = [jnp.where(along_x, p, 0.0) for p in parts] + [jnp.where(along_x, 0.0, p) for p in parts]
        got = dot(jnp.concatenate(parts, axis=0).astype(BF16), place)
        got = [got[LEV * i : LEV * (i + 1)] for i in range(len(parts))]
        got = [got[i] + got[i + 1] for i in range(0, len(got), 2)]
        return [(got[i], got[i + len(pairs)]) for i in range(len(pairs))]

    def shifts(h, halo):
        halo_x, halo_y = halo
        return (
            jnp.where(col == TS - 1, halo_x, roll(h, -1)),
            jnp.where(col == 0, halo_x, roll(h, 1)),
            jnp.where(row == TS - 1, halo_y, roll(h, -TS)),
            jnp.where(row == 0, halo_y, roll(h, TS)),
        )

    wind = wind_ref[...]
    east, north = wind[:LEV], wind[LEV:]
    cosine, sine = trig_ref[0:1, :], trig_ref[1:2, :]
    rim = rims_of(wind)
    rim_e, rim_n = rim[:LEV], rim[LEV:]

    c0 = c0 + towards(edge_of, cos0, sin0, rim_e - east0, rim_n - north0)
    ends = (at == 0) | (at == 31)
    c0 = c0 + jnp.where(ends, towards(side_v, cos0, sin0, far_e - east0, far_n - north0), 0.0)
    c1 = c1 + jnp.where(ends, towards(side_v, cos1, sin1, far_qe - own_qe, far_qn - own_qn), 0.0)
    far_c = far_c + towards(far_edge_v, far_cos, far_sin, east0 - far_e, north0 - far_n)

    last_e, last_n = zero, zero
    for index, (spot, side) in enumerate(zip(spots, sides)):
        code = code_of(far[index][0][0], side)
        end = (far[index][1] < 2).astype(jnp.int32) ^ (code & 1)
        corner = corner_of((code >> 1) & 3, end)
        _, low = packet(code >> 3)
        last_e = take(last_e, low, 96 + 4 * corner, spot)
        last_n = take(last_n, low, 112 + 4 * corner, spot)
    far_c = far_c + towards(far_side_v, far_cos, far_sin, last_e - far_e, last_n - far_n)
    after = jnp.where(at == 31, far_c, roll(c0, -1))
    before = jnp.where(at == 0, far_c, roll(c0, 1))
    s0 = c0 + 0.2 * (c1 + after + before - 4.0 * c0)
    halo_e, halo_n, halo_c, halo_s = placed(
        [(east_hi, east_lo), (north_hi, north_lo), halves(c0), halves(s0)]
    )

    ex, exm, ey, eym = shifts(east, halo_e)
    nx, nxm, ny, nym = shifts(north, halo_n)
    along = cosine * (0.5 * (east + ey)) + sine * (0.5 * (north + ny))
    across = -sine * (0.5 * (east + ex)) + cosine * (0.5 * (north + nx))
    dgrid_ref[...] = jnp.concatenate([along, across], axis=0).astype(BF16)
    vortex = cosine * (0.5 * (nx - nxm) - 0.5 * (ey - eym)) - sine * (0.5 * (ex - exm) + 0.5 * (ny - nym))
    halo_s = tuple(h + 0.2 * vortex for h in halo_s)
    for halo in (halo_c, halo_s):
        xp, xm, yp, ym = shifts(vortex, halo)
        vortex = vortex + 0.2 * (xp + xm + yp + ym - 4.0 * vortex)
    vortex_ref[...] = vortex


def vmem():
    return pl.BlockSpec(memory_space=pltpu.VMEM)


def smem():
    return pl.BlockSpec(memory_space=pltpu.SMEM)


def shape(dims, kind):
    return jax.ShapeDtypeStruct(dims, kind)


def anywhere():
    return pl.BlockSpec(memory_space=pl.ANY)


def hbm():
    return pl.BlockSpec(memory_space=pltpu.HBM)


def cost(flops, moved):
    return pl.CostEstimate(flops=flops, bytes_accessed=moved, transcendentals=0)


def body(checkpoint, remap_weights, margins, seams, rotation_angle):
    weights = remap_weights[0, 0].reshape(K * SB, CELLS)
    limit = pltpu.CompilerParams(vmem_limit_bytes=16 * MIB)

    def in_hbm(x):
        return pltpu.with_memory_space_constraint(x, pltpu.HBM)

    asked, meta, held = pl.pallas_call(
        ask_kernel,
        out_shape=(
            shape((N_TILE, 1, LANES), jnp.int32),
            shape((LEV, LANES), jnp.int32),
            shape(checkpoint.shape, BF16),
        ),
        in_specs=[hbm()] * 3,
        out_specs=(vmem(),) * 3,
        scratch_shapes=[
            pltpu.SMEM((K,), jnp.int32),
            pltpu.SMEM((3, 1, 4), jnp.int32),
            pltpu.SemaphoreType.DMA((3,)),
        ],
        compiler_params=limit,
        name="ask",
    )(in_hbm(margins[0, 0]), in_hbm(seams.reshape(3, 1, 4)), in_hbm(checkpoint))
    asked = lax.all_to_all(asked, "tile", 0, 0, tiled=True).reshape(N_TILE, LANES)
    blocks = pl.pallas_call(
        select_kernel,
        out_shape=shape((N_TILE, ROWS, CAP * SB), BF16),
        in_specs=[smem(), vmem()],
        out_specs=vmem(),
        compiler_params=limit,
        name="select",
    )(asked, held)
    blocks = lax.all_to_all(blocks, "tile", 0, 0, tiled=True)

    scalars, wind, trig, place, packets = pl.pallas_call(
        remap_kernel,
        out_shape=(
            shape((ROWS - WINDS, CELLS), BF16),
            shape((WINDS, CELLS), F32),
            shape((LEV, CELLS), F32),
            shape((LANES, CELLS), BF16),
            shape((TILES, 16, LANES), BF16),
        ),
        in_specs=[smem(), vmem(), hbm(), hbm()],
        out_specs=(vmem(),) * 5,
        scratch_shapes=[
            pltpu.VMEM((ROWS, K * SB), BF16),
            pltpu.VMEM((K * SB, CELLS), BF16),
            pltpu.VMEM((CELLS, 3 * LANES), BF16),
            pltpu.VMEM((1, CELLS), F32),
            pltpu.SemaphoreType.DMA((K * SB // CHUNK + 1,)),
        ],
        compiler_params=limit,
        cost_estimate=cost(2 * ROWS * K * SB * CELLS, 9 * MIB),
        name="remap",
    )(meta, blocks, in_hbm(weights), in_hbm(rotation_angle[0, 0].reshape(1, CELLS)))
    packets = lax.all_to_all(packets, ("tile", "face"), 0, 0, tiled=True)

    scalars, dgrid, vortex = pl.pallas_call(
        smooth_kernel,
        out_shape=(
            shape((ROWS - WINDS, CELLS), BF16),
            shape((WINDS, CELLS), BF16),
            shape((LEV, CELLS), F32),
        ),
        in_specs=[smem()] + [vmem()] * 5,
        out_specs=(vmem(),) * 3,
        compiler_params=limit,
        name="smooth",
    )(meta, packets, wind, trig, place, scalars)
    return (
        scalars.reshape(1, 1, ROWS - WINDS, CELLS),
        dgrid.reshape(1, 1, WINDS, CELLS),
        vortex.reshape(1, 1, LEV, CELLS),
    )


def solution(mesh):
    placed = (
        P(None, "tile"),
        P("face", "tile", None, None, None),
        P("face", "tile", None),
        P("face", "tile", None, None),
        P("face", "tile", None),
    )
    return jax.shard_map(
        body,
        mesh=mesh,
        in_specs=placed,
        out_specs=(P("face", "tile", None, None),) * 3,
        check_vma=False,
    )
```

```python
import jax
import jax.numpy as jnp
from jax import lax
from jax.experimental import pallas as pl
from jax.experimental.pallas import tpu as pltpu
from jax.sharding import PartitionSpec as P

LEV = 8
FIELDS = 6
TS = 32
CELLS = TS * TS
SB = 256
BLK_DEV = 8
K = 16
CAP = 2
GROUPS = K // CAP
N_TILE = 16
TILES = 128
ROWS = FIELDS * LEV
WINDS = 2 * LEV
LANES = 128
MIB = 1 << 20
CHUNK = 256
F32 = jnp.float32
BF16 = jnp.bfloat16


def iota(shape, dim):
    return lax.broadcasted_iota(jnp.int32, shape, dim)


def dot(a, b, contract=((1,), (0,))):
    return lax.dot_general(a, b, (contract, ((), ())), preferred_element_type=F32)


def halves(x):
    hi = x.astype(BF16).astype(F32)
    return hi, x - hi


def roll(x, shift):
    return pltpu.roll(x, shift % x.shape[1], 1)


def lane_pick(group, values):
    out = jnp.full(group.shape, values[0])
    for index in range(1, len(values)):
        out = jnp.where(group == index, values[index], out)
    return out


def towards(direction, cosine, sine, d_east, d_north):
    a_east = jnp.where(
        direction == 0, -cosine, jnp.where(direction == 1, -sine, jnp.where(direction == 2, cosine, sine))
    )
    a_north = jnp.where(
        direction == 0, -sine, jnp.where(direction == 1, cosine, jnp.where(direction == 2, sine, -cosine))
    )
    return 0.5 * (a_east * d_east + a_north * d_north)


def neighbours_within(h, row, col):
    return (
        jnp.where(col == TS - 1, h, roll(h, -1)),
        jnp.where(col == 0, h, roll(h, 1)),
        jnp.where(row == TS - 1, h, roll(h, -TS)),
        jnp.where(row == 0, h, roll(h, TS)),
    )


def ask_kernel(
    margins_ref, seams_ref, checkpoint_ref, asked_ref, meta_ref, held_ref, margins, seams, sems
):
    copies = [
        pltpu.make_async_copy(margins_ref, margins, sems.at[0]),
        pltpu.make_async_copy(seams_ref, seams, sems.at[1]),
        pltpu.make_async_copy(checkpoint_ref, held_ref, sems.at[2]),
    ]
    for copy in copies:
        copy.start()
    copies[0].wait()
    reader, lane = iota((N_TILE, LANES), 0), iota((N_TILE, LANES), 1)
    asked = jnp.zeros((N_TILE, LANES), jnp.int32)
    for m in range(GROUPS):
        first, second = margins[CAP * m], margins[CAP * m + 1]
        asked = jnp.where(reader == (first >> 3), jnp.where(lane == 0, first, second), asked)
    asked = asked & (BLK_DEV - 1)
    for r in range(N_TILE):
        asked_ref[r] = asked[r : r + 1]

    copies[1].wait()
    level, lane = iota((LEV, LANES), 0), iota((LEV, LANES), 1)
    meta = jnp.zeros((LEV, LANES), jnp.int32)
    for m in range(GROUPS):
        reader = jnp.clip(margins[CAP * m] >> 3, 0, N_TILE - 1)
        meta = jnp.where((level == 0) & (lane == m), reader, meta)
    for kind in range(3):
        for e in range(4):
            meta = jnp.where((level == kind + 1) & (lane == e), seams[kind, 0, e], meta)
    meta_ref[...] = meta
    copies[2].wait()


def slot(tile):
    tile = jnp.clip(tile, 0, TILES - 1)
    return (tile & (N_TILE - 1)) * (TILES // N_TILE) + (tile >> 4)


def select_kernel(asked_ref, held_ref, out_ref):
    asked = asked_ref[...]
    for g in range(N_TILE):
        for j in range(CAP):
            block = asked[g, j] & (BLK_DEV - 1)
            out_ref[g, :, j * SB : (j + 1) * SB] = held_ref[:, pl.ds(pl.multiple_of(block * SB, SB), SB)]


def remap_kernel(
    meta_ref, blocks_ref, weights_ref, angle_ref,
    scalars_ref, wind_ref, trig_ref, place_ref, send_ref,
    chosen, streamed, pick_ref, angle, sems,
):
    angle_copy = pltpu.make_async_copy(angle_ref, angle, sems.at[K * SB // CHUNK])
    angle_copy.start()
    spans = [(k, pl.ds(k, CHUNK)) for k in range(0, K * SB, CHUNK)]
    copies = [
        pltpu.make_async_copy(weights_ref.at[span], streamed.at[span], sems.at[index])
        for index, (k, span) in enumerate(spans)
    ]
    for copy in copies:
        copy.start()
    meta = meta_ref[...]
    for m in range(GROUPS):
        chosen[:, CAP * SB * m : CAP * SB * (m + 1)] = blocks_ref[meta[0, m]]
    total = None

    angle_copy.wait()
    trig_ref[...] = jnp.where((iota((LEV, CELLS), 0) & 1) == 0, jnp.cos(angle[...]), jnp.sin(angle[...]))

    lane = iota((1, 3 * LANES), 1)
    edge, depth, at = (lane >> 6) & 3, (lane >> 5) & 1, lane & 31
    rim_cell = jnp.where(
        edge == 0, (TS - 1 - depth) * TS + at,
        jnp.where(edge == 1, at * TS + TS - 1 - depth, jnp.where(edge == 2, depth * TS + at, at * TS + depth)),
    )
    corner, k = (lane >> 2) & 3, lane & 3
    c_row, c_col = (corner >> 1) * (TS - 1), (corner & 1) * (TS - 1)
    c_row = jnp.where(k == 2, jnp.where(c_row == 0, 1, TS - 2), c_row)
    c_col = jnp.where(k == 1, jnp.where(c_col == 0, 1, TS - 2), c_col)
    corner_cell = jnp.where((lane & 127) >= 96, c_row * TS + c_col, -1)
    taken = jnp.where(lane < 2 * LANES, rim_cell, corner_cell)
    pick_ref[...] = (iota((CELLS, 3 * LANES), 0) == taken).astype(F32).astype(BF16)

    line = iota((LANES, 1), 0)
    line_edge, line_at = line >> 5, line & 31
    flipped = lane_pick(line_edge, [meta[3, e] for e in range(4)]) == 1
    line_at = jnp.where(flipped, TS - 1 - line_at, line_at)
    rim_cell = jnp.where(
        line_edge == 0, (TS - 1) * TS + line_at,
        jnp.where(line_edge == 1, line_at * TS + TS - 1, jnp.where(line_edge == 2, line_at, line_at * TS)),
    )
    place_ref[...] = (iota((LANES, CELLS), 1) == rim_cell).astype(F32).astype(BF16)

    for copy, (k, _) in zip(copies, spans):
        copy.wait()
        part = dot(chosen[:, k : k + CHUNK], streamed[k : k + CHUNK])
        total = part if total is None else total + part
    scalars_ref[...] = total[WINDS:].astype(BF16)
    wind = total[:WINDS]
    wind_ref[...] = wind
    east, north = wind[:LEV], wind[LEV:]

    cell = iota((1, CELLS), 1)
    row, col = cell >> 5, cell & (TS - 1)
    trig = trig_ref[...]
    cosine, sine = trig[0:1], trig[1:2]
    ex, exm, ey, eym = neighbours_within(east, row, col)
    nx, nxm, ny, nym = neighbours_within(north, row, col)
    curl = cosine * (0.5 * (nx - nxm) - 0.5 * (ey - eym)) - sine * (0.5 * (ex - exm) + 0.5 * (ny - nym))

    hi, lo = halves(jnp.concatenate([east, north, curl, trig], axis=0))
    got = dot(jnp.concatenate([hi, lo], axis=0).astype(BF16), pick_ref[...])

    lane = iota((LEV, LANES), 1)
    level = iota((LEV, LANES), 0)
    group = lane >> 5
    corners = got[:, 2 * LANES :]
    common_top = jnp.where((level == 5) | (level == 6), corners[24:32], 0.0)
    for e in range(4):
        tile = meta[1, e].astype(F32)
        code = (meta[2, e] * 2 + meta[3, e]).astype(F32)
        common_top = jnp.where((level == 4) & (lane == 96 + e), tile, common_top)
        common_top = jnp.where((level == 4) & (lane == 100 + e), code, common_top)
    common_low = jnp.where(
        lane >= 112, corners[8:16], jnp.where((lane & 3) == 3, corners[16:24], corners[0:8])
    )
    common_low = jnp.where(group == 3, common_low, 0.0)
    common = jnp.concatenate([common_top, common_low], axis=0).astype(BF16)
    for t in range(TILES):
        send_ref[t] = common
    for e in range(4):
        rim = roll(got[:, LANES * (e // 2) : LANES * (e // 2 + 1)], -64 * (e % 2))
        top = jnp.where(
            group == 0, rim[0:8],
            jnp.where(group == 1, roll(rim[32:40], 32), jnp.where(group == 2, roll(rim[16:24], 64), common_top)),
        )
        top = jnp.where((group == 3) & (level < 2), roll(rim[24:32], 96), top)
        top = jnp.where((group == 3) & ((level == 2) | (level == 3)), roll(rim[24:32], 64), top)
        low = jnp.where(
            group == 0, rim[8:16],
            jnp.where(group == 1, roll(rim[40:48], 32), jnp.where(group == 2, roll(rim[16:24], 32), common_low)),
        )
        send_ref[slot(meta[1, e])] = jnp.concatenate([top, low], axis=0).astype(BF16)


def smooth_kernel(
    meta_ref, packets_ref, wind_ref, trig_ref, place_ref, scalars_ref, scalars_out_ref, dgrid_ref, vortex_ref
):
    meta = meta_ref[...]

    def packet(tile):
        both = packets_ref[slot(tile)].astype(F32)
        return both[:LEV], both[LEV:]

    def corner_of(edge, end):
        return jnp.where((edge & 1) == 0, jnp.where(edge == 0, 2, 0) + end, 2 * end + jnp.where(edge == 1, 1, 0))

    scalars_out_ref[...] = scalars_ref[...]
    lane = iota((LEV, LANES), 1)
    group = lane >> 5
    at = lane & 31
    zero = jnp.zeros((LEV, LANES), F32)
    edges = [meta[2, e] for e in range(4)]
    near = [packet(meta[1, e]) for e in range(4)]

    def code_of(top, edge):
        codes = pltpu.roll(top * 8.0 + roll(top, -4), (LANES - 96 - edge) & 127, 1)
        return codes[4, 0].astype(jnp.int32)

    def strip(half, source):
        out = roll(near[0][half], -32 * source)
        for e in range(1, 4):
            out = jnp.where(group == e, roll(near[e][half], 32 * (e - source)), out)
        return out

    east_hi, east_lo, c0, misc = [strip(0, s) for s in range(4)]
    north_hi, north_lo, c1 = [strip(1, s) for s in range(3)]
    east0, north0 = east_hi + east_lo, north_hi + north_lo
    cos0, sin0, cos1, sin1 = [misc[r : r + 1] for r in range(4)]
    lane1 = iota((1, LANES), 1)
    edge_of = lane_pick(lane1 >> 5, edges)

    spots = [(e, end) for e in range(4) for end in range(2)]

    def take(into, vector, source, spot):
        goal = 32 * spot[0] + 31 * spot[1]
        return jnp.where(lane == goal, pltpu.roll(vector, (goal + LANES - source) & 127, 1), into)

    def mark(into, value, spot):
        return jnp.where(lane1 == 32 * spot[0] + 31 * spot[1], value, into)

    own_qe, own_qn = zero, zero
    side_v = jnp.zeros((1, LANES), jnp.int32)
    sides = []
    for spot in spots:
        e, end = spot
        even = (edges[e] & 1) == 0
        side = jnp.where(even, 1 if end else 3, 0 if end else 2)
        corner = corner_of(edges[e], end)
        beside = jnp.where(even, 2, 1)
        own_qe = take(own_qe, near[e][1], 96 + 4 * corner + beside, spot)
        own_qn = take(own_qn, near[e][1], 112 + 4 * corner + beside, spot)
        side_v = mark(side_v, side, spot)
        sides.append(side)

    far = []
    for spot, side in zip(spots, sides):
        code = code_of(near[spot[0]][0], side)
        end = (edges[spot[0]] < 2).astype(jnp.int32) ^ (code & 1)
        far.append((packet(code >> 3), (code >> 1) & 3, end))

    far_e, far_n, far_qe, far_qn, far_c, far_cos, far_sin = (zero,) * 7
    far_edge_v, far_side_v = jnp.zeros_like(side_v), jnp.zeros_like(side_v)
    sides = []
    for spot, ((top, low), edge, end) in zip(spots, far):
        corner = corner_of(edge, end)
        even = (edge & 1) == 0
        beside = jnp.where(even, 1, 2)
        side = jnp.where(even, jnp.where(end == 1, 1, 3), jnp.where(end == 1, 0, 2))
        far_e = take(far_e, low, 96 + 4 * corner, spot)
        far_n = take(far_n, low, 112 + 4 * corner, spot)
        far_qe = take(far_qe, low, 96 + 4 * corner + beside, spot)
        far_qn = take(far_qn, low, 112 + 4 * corner + beside, spot)
        far_c = take(far_c, low, 96 + 4 * corner + 3, spot)
        trig = take(zero, top, 96 + 4 * corner, spot)
        far_cos, far_sin = far_cos + trig[6:7], far_sin + trig[5:6]
        far_edge_v = mark(far_edge_v, edge, spot)
        far_side_v = mark(far_side_v, side, spot)
        sides.append(side)

    place = place_ref[...]
    cell = iota((1, CELLS), 1)
    row, col = cell >> 5, cell & (TS - 1)
    along_x = (group & 1) == 1

    def rims_of(fields):
        hi, lo = halves(fields)
        got = dot(jnp.concatenate([hi, lo], axis=0).astype(BF16), place, ((1,), (1,)))
        return got[: fields.shape[0]] + got[fields.shape[0] :]

    def placed(pairs):
        parts = [p for pair in pairs for p in pair]
        parts = [jnp.where(along_x, p, 0.0) for p in parts] + [jnp.where(along_x, 0.0, p) for p in parts]
        got = dot(jnp.concatenate(parts, axis=0).astype(BF16), place)
        got = [got[LEV * i : LEV * (i + 1)] for i in range(len(parts))]
        got = [got[i] + got[i + 1] for i in range(0, len(got), 2)]
        return [(got[i], got[i + len(pairs)]) for i in range(len(pairs))]

    def shifts(h, halo):
        halo_x, halo_y = halo
        return (
            jnp.where(col == TS - 1, halo_x, roll(h, -1)),
            jnp.where(col == 0, halo_x, roll(h, 1)),
            jnp.where(row == TS - 1, halo_y, roll(h, -TS)),
            jnp.where(row == 0, halo_y, roll(h, TS)),
        )

    wind = wind_ref[...]
    east, north = wind[:LEV], wind[LEV:]
    cosine, sine = trig_ref[0:1, :], trig_ref[1:2, :]
    rim = rims_of(wind)
    rim_e, rim_n = rim[:LEV], rim[LEV:]

    c0 = c0 + towards(edge_of, cos0, sin0, rim_e - east0, rim_n - north0)
    ends = (at == 0) | (at == 31)
    c0 = c0 + jnp.where(ends, towards(side_v, cos0, sin0, far_e - east0, far_n - north0), 0.0)
    c1 = c1 + jnp.where(ends, towards(side_v, cos1, sin1, far_qe - own_qe, far_qn - own_qn), 0.0)
    far_c = far_c + towards(far_edge_v, far_cos, far_sin, east0 - far_e, north0 - far_n)

    last_e, last_n = zero, zero
    for index, (spot, side) in enumerate(zip(spots, sides)):
        code = code_of(far[index][0][0], side)
        end = (far[index][1] < 2).astype(jnp.int32) ^ (code & 1)
        corner = corner_of((code >> 1) & 3, end)
        _, low = packet(code >> 3)
        last_e = take(last_e, low, 96 + 4 * corner, spot)
        last_n = take(last_n, low, 112 + 4 * corner, spot)
    far_c = far_c + towards(far_side_v, far_cos, far_sin, last_e - far_e, last_n - far_n)
    after = jnp.where(at == 31, far_c, roll(c0, -1))
    before = jnp.where(at == 0, far_c, roll(c0, 1))
    s0 = c0 + 0.2 * (c1 + after + before - 4.0 * c0)
    halo_e, halo_n, halo_c, halo_s = placed(
        [(east_hi, east_lo), (north_hi, north_lo), halves(c0), halves(s0)]
    )

    ex, exm, ey, eym = shifts(east, halo_e)
    nx, nxm, ny, nym = shifts(north, halo_n)
    along = cosine * (0.5 * (east + ey)) + sine * (0.5 * (north + ny))
    across = -sine * (0.5 * (east + ex)) + cosine * (0.5 * (north + nx))
    dgrid_ref[...] = jnp.concatenate([along, across], axis=0).astype(BF16)
    vortex = cosine * (0.5 * (nx - nxm) - 0.5 * (ey - eym)) - sine * (0.5 * (ex - exm) + 0.5 * (ny - nym))
    halo_s = tuple(h + 0.2 * vortex for h in halo_s)
    for halo in (halo_c, halo_s):
        xp, xm, yp, ym = shifts(vortex, halo)
        vortex = vortex + 0.2 * (xp + xm + yp + ym - 4.0 * vortex)
    vortex_ref[...] = vortex


def vmem():
    return pl.BlockSpec(memory_space=pltpu.VMEM)


def shape(dims, kind):
    return jax.ShapeDtypeStruct(dims, kind)


def hbm():
    return pl.BlockSpec(memory_space=pltpu.HBM)


def cost(flops, moved):
    return pl.CostEstimate(flops=flops, bytes_accessed=moved, transcendentals=0)


def body(checkpoint, remap_weights, margins, seams, rotation_angle):
    weights = remap_weights[0, 0].reshape(K * SB, CELLS)
    limit = pltpu.CompilerParams(vmem_limit_bytes=16 * MIB)

    def in_hbm(x):
        return pltpu.with_memory_space_constraint(x, pltpu.HBM)

    asked, meta, held = pl.pallas_call(
        ask_kernel,
        out_shape=(
            shape((N_TILE, 1, LANES), jnp.int32),
            shape((LEV, LANES), jnp.int32),
            shape(checkpoint.shape, BF16),
        ),
        in_specs=[hbm()] * 3,
        out_specs=(vmem(),) * 3,
        scratch_shapes=[
            pltpu.SMEM((K,), jnp.int32),
            pltpu.SMEM((3, 1, 4), jnp.int32),
            pltpu.SemaphoreType.DMA((3,)),
        ],
        compiler_params=limit,
        name="ask",
    )(in_hbm(margins[0, 0]), in_hbm(seams.reshape(3, 1, 4)), in_hbm(checkpoint))
    asked = lax.all_to_all(asked, "tile", 0, 0, tiled=True).reshape(N_TILE, LANES)
    blocks = pl.pallas_call(
        select_kernel,
        out_shape=shape((N_TILE, ROWS, CAP * SB), BF16),
        in_specs=[vmem(), vmem()],
        out_specs=vmem(),
        compiler_params=limit,
        name="select",
    )(asked, held)
    blocks = lax.all_to_all(blocks, "tile", 0, 0, tiled=True)

    scalars, wind, trig, place, packets = pl.pallas_call(
        remap_kernel,
        out_shape=(
            shape((ROWS - WINDS, CELLS), BF16),
            shape((WINDS, CELLS), F32),
            shape((LEV, CELLS), F32),
            shape((LANES, CELLS), BF16),
            shape((TILES, 16, LANES), BF16),
        ),
        in_specs=[vmem(), vmem(), hbm(), hbm()],
        out_specs=(vmem(),) * 5,
        scratch_shapes=[
            pltpu.VMEM((ROWS, K * SB), BF16),
            pltpu.VMEM((K * SB, CELLS), BF16),
            pltpu.VMEM((CELLS, 3 * LANES), BF16),
            pltpu.VMEM((1, CELLS), F32),
            pltpu.SemaphoreType.DMA((K * SB // CHUNK + 1,)),
        ],
        compiler_params=limit,
        cost_estimate=cost(2 * ROWS * K * SB * CELLS, 9 * MIB),
        name="remap",
    )(meta, blocks, in_hbm(weights), in_hbm(rotation_angle[0, 0].reshape(1, CELLS)))
    packets = lax.all_to_all(packets, ("tile", "face"), 0, 0, tiled=True)

    scalars, dgrid, vortex = pl.pallas_call(
        smooth_kernel,
        out_shape=(
            shape((ROWS - WINDS, CELLS), BF16),
            shape((WINDS, CELLS), BF16),
            shape((LEV, CELLS), F32),
        ),
        in_specs=[vmem()] * 6,
        out_specs=(vmem(),) * 3,
        compiler_params=limit,
        name="smooth",
    )(meta, packets, wind, trig, place, scalars)
    return (
        scalars.reshape(1, 1, ROWS - WINDS, CELLS),
        dgrid.reshape(1, 1, WINDS, CELLS),
        vortex.reshape(1, 1, LEV, CELLS),
    )


def solution(mesh):
    placed = (
        P(None, "tile"),
        P("face", "tile", None, None, None),
        P("face", "tile", None),
        P("face", "tile", None, None),
        P("face", "tile", None),
    )
    return jax.shard_map(
        body,
        mesh=mesh,
        in_specs=placed,
        out_specs=(P("face", "tile", None, None),) * 3,
        check_vma=False,
    )
```

```python
import jax
import jax.numpy as jnp
from jax import lax
from jax.experimental import pallas as pl
from jax.experimental.pallas import tpu as pltpu
from jax.sharding import PartitionSpec as P

LEV = 8
FIELDS = 6
TS = 32
CELLS = TS * TS
SB = 256
BLK_DEV = 8
K = 16
CAP = 2
GROUPS = K // CAP
N_TILE = 16
TILES = 128
ROWS = FIELDS * LEV
WINDS = 2 * LEV
LANES = 128
MIB = 1 << 20
CHUNK = 256
F32 = jnp.float32
BF16 = jnp.bfloat16


def iota(shape, dim):
    return lax.broadcasted_iota(jnp.int32, shape, dim)


def dot(a, b, contract=((1,), (0,))):
    return lax.dot_general(a, b, (contract, ((), ())), preferred_element_type=F32)


def halves(x):
    hi = x.astype(BF16).astype(F32)
    return hi, x - hi


def roll(x, shift):
    return pltpu.roll(x, shift % x.shape[1], 1)


def lane_pick(group, values):
    out = jnp.full(group.shape, values[0])
    for index in range(1, len(values)):
        out = jnp.where(group == index, values[index], out)
    return out


def towards(direction, cosine, sine, d_east, d_north):
    a_east = jnp.where(
        direction == 0, -cosine, jnp.where(direction == 1, -sine, jnp.where(direction == 2, cosine, sine))
    )
    a_north = jnp.where(
        direction == 0, -sine, jnp.where(direction == 1, cosine, jnp.where(direction == 2, sine, -cosine))
    )
    return 0.5 * (a_east * d_east + a_north * d_north)


def neighbours_within(h, row, col):
    return (
        jnp.where(col == TS - 1, h, roll(h, -1)),
        jnp.where(col == 0, h, roll(h, 1)),
        jnp.where(row == TS - 1, h, roll(h, -TS)),
        jnp.where(row == 0, h, roll(h, TS)),
    )


def ask_kernel(
    margins_ref, seams_ref, checkpoint_ref, asked_ref, meta_ref, held_ref, margins, seams, sems
):
    copies = [
        pltpu.make_async_copy(margins_ref, margins, sems.at[0]),
        pltpu.make_async_copy(seams_ref, seams, sems.at[1]),
        pltpu.make_async_copy(checkpoint_ref, held_ref, sems.at[2]),
    ]
    for copy in copies:
        copy.start()
    copies[0].wait()
    reader, lane = iota((N_TILE, LANES), 0), iota((N_TILE, LANES), 1)
    asked = jnp.zeros((N_TILE, LANES), jnp.int32)
    for m in range(GROUPS):
        first, second = margins[CAP * m], margins[CAP * m + 1]
        asked = jnp.where(reader == (first >> 3), jnp.where(lane == 0, first, second), asked)
    asked = asked & (BLK_DEV - 1)
    for r in range(N_TILE):
        asked_ref[r] = asked[r : r + 1]

    copies[1].wait()
    level, lane = iota((LEV, LANES), 0), iota((LEV, LANES), 1)
    meta = jnp.zeros((LEV, LANES), jnp.int32)
    for m in range(GROUPS):
        reader = jnp.clip(margins[CAP * m] >> 3, 0, N_TILE - 1)
        meta = jnp.where((level == 0) & (lane == m), reader, meta)
    for kind in range(3):
        for e in range(4):
            meta = jnp.where((level == kind + 1) & (lane == e), seams[kind, 0, e], meta)
    meta_ref[...] = meta
    copies[2].wait()


def slot(tile):
    tile = jnp.clip(tile, 0, TILES - 1)
    return (tile & (N_TILE - 1)) * (TILES // N_TILE) + (tile >> 4)


def select_kernel(asked_ref, held_ref, out_ref):
    asked = asked_ref[...]
    for g in range(N_TILE):
        for j in range(CAP):
            block = asked[g, j] & (BLK_DEV - 1)
            out_ref[g, :, j * SB : (j + 1) * SB] = held_ref[:, pl.ds(pl.multiple_of(block * SB, SB), SB)]


def remap_kernel(
    meta_ref, blocks_ref, weights_ref, angle_ref,
    scalars_ref, wind_ref, trig_ref, place_ref, send_ref,
    chosen, streamed, pick_ref, angle, sems,
):
    angle_copy = pltpu.make_async_copy(angle_ref, angle, sems.at[K * SB // CHUNK])
    angle_copy.start()
    spans = [(k, pl.ds(k, CHUNK)) for k in range(0, K * SB, CHUNK)]
    copies = [
        pltpu.make_async_copy(weights_ref.at[span], streamed.at[span], sems.at[index])
        for index, (k, span) in enumerate(spans)
    ]
    for copy in copies:
        copy.start()
    meta = meta_ref[...]
    for m in range(GROUPS):
        chosen[:, CAP * SB * m : CAP * SB * (m + 1)] = blocks_ref[meta[0, m]]
    total = None

    angle_copy.wait()
    trig_ref[...] = jnp.where((iota((LEV, CELLS), 0) & 1) == 0, jnp.cos(angle[...]), jnp.sin(angle[...]))

    lane = iota((1, 2 * LANES), 1)
    depth, at = (lane >> 5) & 1, lane & 31
    column_cell = at * TS + jnp.where((lane >> 6) == 0, TS - 1 - depth, depth)
    corner, k = (lane >> 2) & 3, lane & 3
    c_row, c_col = (corner >> 1) * (TS - 1), (corner & 1) * (TS - 1)
    c_row = jnp.where(k == 2, jnp.where(c_row == 0, 1, TS - 2), c_row)
    c_col = jnp.where(k == 1, jnp.where(c_col == 0, 1, TS - 2), c_col)
    corner_cell = jnp.where((lane & 127) >= 96, c_row * TS + c_col, -1)
    taken = jnp.where(lane < LANES, column_cell, corner_cell)
    pick_ref[...] = (iota((CELLS, 2 * LANES), 0) == taken).astype(F32).astype(BF16)

    line = iota((LANES, 1), 0)
    line_edge, line_at = line >> 5, line & 31
    flipped = lane_pick(line_edge, [meta[3, e] for e in range(4)]) == 1
    line_at = jnp.where(flipped, TS - 1 - line_at, line_at)
    rim_cell = jnp.where(
        line_edge == 0, (TS - 1) * TS + line_at,
        jnp.where(line_edge == 1, line_at * TS + TS - 1, jnp.where(line_edge == 2, line_at, line_at * TS)),
    )
    place_ref[...] = (iota((LANES, CELLS), 1) == rim_cell).astype(F32).astype(BF16)

    for copy, (k, _) in zip(copies, spans):
        copy.wait()
        part = dot(chosen[:, k : k + CHUNK], streamed[k : k + CHUNK])
        total = part if total is None else total + part
    scalars_ref[...] = total[WINDS:].astype(BF16)
    wind = total[:WINDS]
    wind_ref[...] = wind
    east, north = wind[:LEV], wind[LEV:]

    cell = iota((1, CELLS), 1)
    row, col = cell >> 5, cell & (TS - 1)
    trig = trig_ref[...]
    cosine, sine = trig[0:1], trig[1:2]
    ex, exm, ey, eym = neighbours_within(east, row, col)
    nx, nxm, ny, nym = neighbours_within(north, row, col)
    curl = cosine * (0.5 * (nx - nxm) - 0.5 * (ey - eym)) - sine * (0.5 * (ex - exm) + 0.5 * (ny - nym))

    hi, lo = halves(jnp.concatenate([east, north, curl, trig], axis=0))
    both = jnp.concatenate([hi, lo], axis=0)
    got = dot(both.astype(BF16), pick_ref[...])

    lane = iota((LEV, LANES), 1)
    level = iota((LEV, LANES), 0)
    group = lane >> 5
    corners = got[:, LANES:]
    common_top = jnp.where((level == 5) | (level == 6), corners[24:32], 0.0)
    for e in range(4):
        tile = meta[1, e].astype(F32)
        code = (meta[2, e] * 2 + meta[3, e]).astype(F32)
        common_top = jnp.where((level == 4) & (lane == 96 + e), tile, common_top)
        common_top = jnp.where((level == 4) & (lane == 100 + e), code, common_top)
    common_low = jnp.where(
        lane >= 112, corners[8:16], jnp.where((lane & 3) == 3, corners[16:24], corners[0:8])
    )
    common_low = jnp.where(group == 3, common_low, 0.0)
    common = jnp.concatenate([common_top, common_low], axis=0).astype(BF16)
    for t in range(TILES):
        send_ref[t] = common
    sources = [
        (both[:, CELLS - LANES :], 96, 64),
        (got[:, :LANES], 0, 32),
        (both[:, :LANES], 0, 32),
        (got[:, :LANES], 64, 96),
    ]
    for e, (rim, at0, at1) in enumerate(sources):

        def to(goal, rows, start):
            return rim[rows] if goal == start else roll(rim[rows], goal - start)

        east_rows, north_rows, curl_rows, trig_rows = (slice(8 * i, 8 * i + 8) for i in range(4))
        east_low, north_low = slice(32, 40), slice(40, 48)
        top = jnp.where(group == 2, to(64, curl_rows, at0), common_top)
        top = jnp.where(group == 0, to(0, east_rows, at0), jnp.where(group == 1, to(32, east_low, at0), top))
        top = jnp.where((group == 3) & (level < 2), to(96, trig_rows, at0), top)
        top = jnp.where((group == 3) & ((level == 2) | (level == 3)), to(96, trig_rows, at1), top)
        low = jnp.where(group == 2, to(64, curl_rows, at1), common_low)
        low = jnp.where(group == 0, to(0, north_rows, at0), jnp.where(group == 1, to(32, north_low, at0), low))
        send_ref[slot(meta[1, e])] = jnp.concatenate([top, low], axis=0).astype(BF16)


def smooth_kernel(
    meta_ref, packets_ref, wind_ref, trig_ref, place_ref, scalars_ref, scalars_out_ref, dgrid_ref, vortex_ref
):
    meta = meta_ref[...]

    def packet(tile):
        both = packets_ref[slot(tile)].astype(F32)
        return both[:LEV], both[LEV:]

    def corner_of(edge, end):
        return jnp.where((edge & 1) == 0, jnp.where(edge == 0, 2, 0) + end, 2 * end + jnp.where(edge == 1, 1, 0))

    scalars_out_ref[...] = scalars_ref[...]
    lane = iota((LEV, LANES), 1)
    group = lane >> 5
    at = lane & 31
    zero = jnp.zeros((LEV, LANES), F32)
    edges = [meta[2, e] for e in range(4)]
    near = [packet(meta[1, e]) for e in range(4)]

    def code_of(top, edge):
        codes = pltpu.roll(top * 8.0 + roll(top, -4), (LANES - 96 - edge) & 127, 1)
        return codes[4, 0].astype(jnp.int32)

    def strip(half, source):
        out = roll(near[0][half], -32 * source)
        for e in range(1, 4):
            out = jnp.where(group == e, roll(near[e][half], 32 * (e - source)), out)
        return out

    east_hi, east_lo, c0, misc = [strip(0, s) for s in range(4)]
    north_hi, north_lo, c1 = [strip(1, s) for s in range(3)]
    east0, north0 = east_hi + east_lo, north_hi + north_lo
    cos0, sin0, cos1, sin1 = [misc[r : r + 1] for r in range(4)]
    lane1 = iota((1, LANES), 1)
    edge_of = lane_pick(lane1 >> 5, edges)

    spots = [(e, end) for e in range(4) for end in range(2)]

    def take(into, vector, source, spot):
        goal = 32 * spot[0] + 31 * spot[1]
        return jnp.where(lane == goal, pltpu.roll(vector, (goal + LANES - source) & 127, 1), into)

    def mark(into, value, spot):
        return jnp.where(lane1 == 32 * spot[0] + 31 * spot[1], value, into)

    own_qe, own_qn = zero, zero
    side_v = jnp.zeros((1, LANES), jnp.int32)
    sides = []
    for spot in spots:
        e, end = spot
        even = (edges[e] & 1) == 0
        side = jnp.where(even, 1 if end else 3, 0 if end else 2)
        corner = corner_of(edges[e], end)
        beside = jnp.where(even, 2, 1)
        own_qe = take(own_qe, near[e][1], 96 + 4 * corner + beside, spot)
        own_qn = take(own_qn, near[e][1], 112 + 4 * corner + beside, spot)
        side_v = mark(side_v, side, spot)
        sides.append(side)

    far = []
    for spot, side in zip(spots, sides):
        code = code_of(near[spot[0]][0], side)
        end = (edges[spot[0]] < 2).astype(jnp.int32) ^ (code & 1)
        far.append((packet(code >> 3), (code >> 1) & 3, end))

    far_e, far_n, far_qe, far_qn, far_c, far_cos, far_sin = (zero,) * 7
    far_edge_v, far_side_v = jnp.zeros_like(side_v), jnp.zeros_like(side_v)
    sides = []
    for spot, ((top, low), edge, end) in zip(spots, far):
        corner = corner_of(edge, end)
        even = (edge & 1) == 0
        beside = jnp.where(even, 1, 2)
        side = jnp.where(even, jnp.where(end == 1, 1, 3), jnp.where(end == 1, 0, 2))
        far_e = take(far_e, low, 96 + 4 * corner, spot)
        far_n = take(far_n, low, 112 + 4 * corner, spot)
        far_qe = take(far_qe, low, 96 + 4 * corner + beside, spot)
        far_qn = take(far_qn, low, 112 + 4 * corner + beside, spot)
        far_c = take(far_c, low, 96 + 4 * corner + 3, spot)
        trig = take(zero, top, 96 + 4 * corner, spot)
        far_cos, far_sin = far_cos + trig[6:7], far_sin + trig[5:6]
        far_edge_v = mark(far_edge_v, edge, spot)
        far_side_v = mark(far_side_v, side, spot)
        sides.append(side)

    place = place_ref[...]
    cell = iota((1, CELLS), 1)
    row, col = cell >> 5, cell & (TS - 1)
    along_x = (group & 1) == 1

    def rims_of(fields):
        hi, lo = halves(fields)
        got = dot(jnp.concatenate([hi, lo], axis=0).astype(BF16), place, ((1,), (1,)))
        return got[: fields.shape[0]] + got[fields.shape[0] :]

    def placed(pairs):
        parts = [p for pair in pairs for p in pair]
        parts = [jnp.where(along_x, p, 0.0) for p in parts] + [jnp.where(along_x, 0.0, p) for p in parts]
        got = dot(jnp.concatenate(parts, axis=0).astype(BF16), place)
        got = [got[LEV * i : LEV * (i + 1)] for i in range(len(parts))]
        got = [got[i] + got[i + 1] for i in range(0, len(got), 2)]
        return [(got[i], got[i + len(pairs)]) for i in range(len(pairs))]

    def shifts(h, halo):
        halo_x, halo_y = halo
        return (
            jnp.where(col == TS - 1, halo_x, roll(h, -1)),
            jnp.where(col == 0, halo_x, roll(h, 1)),
            jnp.where(row == TS - 1, halo_y, roll(h, -TS)),
            jnp.where(row == 0, halo_y, roll(h, TS)),
        )

    wind = wind_ref[...]
    east, north = wind[:LEV], wind[LEV:]
    cosine, sine = trig_ref[0:1, :], trig_ref[1:2, :]
    rim = rims_of(wind)
    rim_e, rim_n = rim[:LEV], rim[LEV:]

    c0 = c0 + towards(edge_of, cos0, sin0, rim_e - east0, rim_n - north0)
    ends = (at == 0) | (at == 31)
    c0 = c0 + jnp.where(ends, towards(side_v, cos0, sin0, far_e - east0, far_n - north0), 0.0)
    c1 = c1 + jnp.where(ends, towards(side_v, cos1, sin1, far_qe - own_qe, far_qn - own_qn), 0.0)
    far_c = far_c + towards(far_edge_v, far_cos, far_sin, east0 - far_e, north0 - far_n)

    last_e, last_n = zero, zero
    for index, (spot, side) in enumerate(zip(spots, sides)):
        code = code_of(far[index][0][0], side)
        end = (far[index][1] < 2).astype(jnp.int32) ^ (code & 1)
        corner = corner_of((code >> 1) & 3, end)
        _, low = packet(code >> 3)
        last_e = take(last_e, low, 96 + 4 * corner, spot)
        last_n = take(last_n, low, 112 + 4 * corner, spot)
    far_c = far_c + towards(far_side_v, far_cos, far_sin, last_e - far_e, last_n - far_n)
    after = jnp.where(at == 31, far_c, roll(c0, -1))
    before = jnp.where(at == 0, far_c, roll(c0, 1))
    s0 = c0 + 0.2 * (c1 + after + before - 4.0 * c0)
    halo_e, halo_n = placed([(east_hi, east_lo), (north_hi, north_lo)])
    halo_c, halo_s = placed([halves(c0), halves(s0)])

    ex, exm, ey, eym = shifts(east, halo_e)
    nx, nxm, ny, nym = shifts(north, halo_n)
    along = cosine * (0.5 * (east + ey)) + sine * (0.5 * (north + ny))
    across = -sine * (0.5 * (east + ex)) + cosine * (0.5 * (north + nx))
    dgrid_ref[...] = jnp.concatenate([along, across], axis=0).astype(BF16)
    vortex = cosine * (0.5 * (nx - nxm) - 0.5 * (ey - eym)) - sine * (0.5 * (ex - exm) + 0.5 * (ny - nym))
    halo_s = tuple(h + 0.2 * vortex for h in halo_s)
    for halo in (halo_c, halo_s):
        xp, xm, yp, ym = shifts(vortex, halo)
        vortex = vortex + 0.2 * (xp + xm + yp + ym - 4.0 * vortex)
    vortex_ref[...] = vortex


def vmem():
    return pl.BlockSpec(memory_space=pltpu.VMEM)


def shape(dims, kind):
    return jax.ShapeDtypeStruct(dims, kind)


def hbm():
    return pl.BlockSpec(memory_space=pltpu.HBM)


def cost(flops, moved):
    return pl.CostEstimate(flops=flops, bytes_accessed=moved, transcendentals=0)


def body(checkpoint, remap_weights, margins, seams, rotation_angle):
    weights = remap_weights[0, 0].reshape(K * SB, CELLS)
    limit = pltpu.CompilerParams(vmem_limit_bytes=16 * MIB)

    def in_hbm(x):
        return pltpu.with_memory_space_constraint(x, pltpu.HBM)

    asked, meta, held = pl.pallas_call(
        ask_kernel,
        out_shape=(
            shape((N_TILE, 1, LANES), jnp.int32),
            shape((LEV, LANES), jnp.int32),
            shape(checkpoint.shape, BF16),
        ),
        in_specs=[hbm()] * 3,
        out_specs=(vmem(),) * 3,
        scratch_shapes=[
            pltpu.SMEM((K,), jnp.int32),
            pltpu.SMEM((3, 1, 4), jnp.int32),
            pltpu.SemaphoreType.DMA((3,)),
        ],
        compiler_params=limit,
        name="ask",
    )(in_hbm(margins[0, 0]), in_hbm(seams.reshape(3, 1, 4)), in_hbm(checkpoint))
    asked = lax.all_to_all(asked, "tile", 0, 0, tiled=True).reshape(N_TILE, LANES)
    blocks = pl.pallas_call(
        select_kernel,
        out_shape=shape((N_TILE, ROWS, CAP * SB), BF16),
        in_specs=[vmem(), vmem()],
        out_specs=vmem(),
        compiler_params=limit,
        name="select",
    )(asked, held)
    blocks = lax.all_to_all(blocks, "tile", 0, 0, tiled=True)

    scalars, wind, trig, place, packets = pl.pallas_call(
        remap_kernel,
        out_shape=(
            shape((ROWS - WINDS, CELLS), BF16),
            shape((WINDS, CELLS), F32),
            shape((LEV, CELLS), F32),
            shape((LANES, CELLS), BF16),
            shape((TILES, 16, LANES), BF16),
        ),
        in_specs=[vmem(), vmem(), hbm(), hbm()],
        out_specs=(vmem(),) * 5,
        scratch_shapes=[
            pltpu.VMEM((ROWS, K * SB), BF16),
            pltpu.VMEM((K * SB, CELLS), BF16),
            pltpu.VMEM((CELLS, 2 * LANES), BF16),
            pltpu.VMEM((1, CELLS), F32),
            pltpu.SemaphoreType.DMA((K * SB // CHUNK + 1,)),
        ],
        compiler_params=limit,
        cost_estimate=cost(2 * ROWS * K * SB * CELLS, 9 * MIB),
        name="remap",
    )(meta, blocks, in_hbm(weights), in_hbm(rotation_angle[0, 0].reshape(1, CELLS)))
    packets = lax.all_to_all(packets, ("tile", "face"), 0, 0, tiled=True)

    scalars, dgrid, vortex = pl.pallas_call(
        smooth_kernel,
        out_shape=(
            shape((ROWS - WINDS, CELLS), BF16),
            shape((WINDS, CELLS), BF16),
            shape((LEV, CELLS), F32),
        ),
        in_specs=[vmem()] * 6,
        out_specs=(vmem(),) * 3,
        compiler_params=limit,
        name="smooth",
    )(meta, packets, wind, trig, place, scalars)
    return (
        scalars.reshape(1, 1, ROWS - WINDS, CELLS),
        dgrid.reshape(1, 1, WINDS, CELLS),
        vortex.reshape(1, 1, LEV, CELLS),
    )


def solution(mesh):
    placed = (
        P(None, "tile"),
        P("face", "tile", None, None, None),
        P("face", "tile", None),
        P("face", "tile", None, None),
        P("face", "tile", None),
    )
    return jax.shard_map(
        body,
        mesh=mesh,
        in_specs=placed,
        out_specs=(P("face", "tile", None, None),) * 3,
        check_vma=False,
    )
```

```python
import jax
import jax.numpy as jnp
from jax import lax
from jax.experimental import pallas as pl
from jax.experimental.pallas import tpu as pltpu
from jax.sharding import PartitionSpec as P

LEV = 8
FIELDS = 6
TS = 32
CELLS = TS * TS
SB = 256
BLK_DEV = 8
K = 16
CAP = 2
GROUPS = K // CAP
N_TILE = 16
TILES = 128
ROWS = FIELDS * LEV
WINDS = 2 * LEV
LANES = 128
MIB = 1 << 20
CHUNK = 256
F32 = jnp.float32
BF16 = jnp.bfloat16


def iota(shape, dim):
    return lax.broadcasted_iota(jnp.int32, shape, dim)


def dot(a, b, contract=((1,), (0,))):
    return lax.dot_general(a, b, (contract, ((), ())), preferred_element_type=F32)


def halves(x):
    hi = x.astype(BF16).astype(F32)
    return hi, x - hi


def roll(x, shift):
    return pltpu.roll(x, shift % x.shape[1], 1)


def lane_pick(group, values):
    out = jnp.full(group.shape, values[0])
    for index in range(1, len(values)):
        out = jnp.where(group == index, values[index], out)
    return out


def towards(direction, cosine, sine, d_east, d_north):
    a_east = jnp.where(
        direction == 0, -cosine, jnp.where(direction == 1, -sine, jnp.where(direction == 2, cosine, sine))
    )
    a_north = jnp.where(
        direction == 0, -sine, jnp.where(direction == 1, cosine, jnp.where(direction == 2, sine, -cosine))
    )
    return 0.5 * (a_east * d_east + a_north * d_north)


def neighbours_within(h, row, col):
    return (
        jnp.where(col == TS - 1, h, roll(h, -1)),
        jnp.where(col == 0, h, roll(h, 1)),
        jnp.where(row == TS - 1, h, roll(h, -TS)),
        jnp.where(row == 0, h, roll(h, TS)),
    )


def ask_kernel(
    margins_ref, seams_ref, checkpoint_ref, asked_ref, meta_ref, held_ref, margins, seams, sems
):
    copies = [
        pltpu.make_async_copy(margins_ref, margins, sems.at[0]),
        pltpu.make_async_copy(seams_ref, seams, sems.at[1]),
        pltpu.make_async_copy(checkpoint_ref, held_ref, sems.at[2]),
    ]
    for copy in copies:
        copy.start()
    copies[0].wait()
    reader, lane = iota((N_TILE, LANES), 0), iota((N_TILE, LANES), 1)
    asked = jnp.zeros((N_TILE, LANES), jnp.int32)
    for m in range(GROUPS):
        first, second = margins[CAP * m], margins[CAP * m + 1]
        asked = jnp.where(reader == (first >> 3), jnp.where(lane == 0, first, second), asked)
    asked = asked & (BLK_DEV - 1)
    for r in range(N_TILE):
        asked_ref[r] = asked[r : r + 1]

    copies[1].wait()
    level, lane = iota((LEV, LANES), 0), iota((LEV, LANES), 1)
    meta = jnp.zeros((LEV, LANES), jnp.int32)
    for m in range(GROUPS):
        reader = jnp.clip(margins[CAP * m] >> 3, 0, N_TILE - 1)
        meta = jnp.where((level == 0) & (lane == m), reader, meta)
    for kind in range(3):
        for e in range(4):
            meta = jnp.where((level == kind + 1) & (lane == e), seams[kind, 0, e], meta)
    meta_ref[...] = meta
    copies[2].wait()


def slot_bits(tile):
    y, z = (tile >> 4) & 3, (tile >> 1) & 3
    return (y << 5) | (z << 3) | ((tile >> 6) << 2) | (((tile >> 3) & 1) << 1) | (tile & 1)


def slot(tile):
    return slot_bits(jnp.clip(tile, 0, TILES - 1))


def select_kernel(asked_ref, held_ref, out_ref):
    asked = asked_ref[...]
    for g in range(N_TILE):
        for j in range(CAP):
            block = asked[g, j] & (BLK_DEV - 1)
            out_ref[g, :, j * SB : (j + 1) * SB] = held_ref[:, pl.ds(pl.multiple_of(block * SB, SB), SB)]


def remap_kernel(
    meta_ref, blocks_ref, weights_ref, angle_ref,
    scalars_ref, wind_ref, trig_ref, place_ref, send_ref,
    chosen, streamed, pick_ref, angle, sems,
):
    angle_copy = pltpu.make_async_copy(angle_ref, angle, sems.at[K * SB // CHUNK])
    angle_copy.start()
    spans = [(k, pl.ds(k, CHUNK)) for k in range(0, K * SB, CHUNK)]
    copies = [
        pltpu.make_async_copy(weights_ref.at[span], streamed.at[span], sems.at[index])
        for index, (k, span) in enumerate(spans)
    ]
    for copy in copies:
        copy.start()
    meta = meta_ref[...]
    for m in range(GROUPS):
        chosen[:, CAP * SB * m : CAP * SB * (m + 1)] = blocks_ref[meta[0, m]]
    total = None

    angle_copy.wait()
    trig_ref[...] = jnp.where((iota((LEV, CELLS), 0) & 1) == 0, jnp.cos(angle[...]), jnp.sin(angle[...]))

    lane = iota((1, 2 * LANES), 1)
    depth, at = (lane >> 5) & 1, lane & 31
    column_cell = at * TS + jnp.where((lane >> 6) == 0, TS - 1 - depth, depth)
    corner, k = (lane >> 2) & 3, lane & 3
    c_row, c_col = (corner >> 1) * (TS - 1), (corner & 1) * (TS - 1)
    c_row = jnp.where(k == 2, jnp.where(c_row == 0, 1, TS - 2), c_row)
    c_col = jnp.where(k == 1, jnp.where(c_col == 0, 1, TS - 2), c_col)
    corner_cell = jnp.where((lane & 127) >= 96, c_row * TS + c_col, -1)
    taken = jnp.where(lane < LANES, column_cell, corner_cell)
    pick_ref[...] = (iota((CELLS, 2 * LANES), 0) == taken).astype(F32).astype(BF16)

    line = iota((LANES, 1), 0)
    line_edge, line_at = line >> 5, line & 31
    flipped = lane_pick(line_edge, [meta[3, e] for e in range(4)]) == 1
    line_at = jnp.where(flipped, TS - 1 - line_at, line_at)
    rim_cell = jnp.where(
        line_edge == 0, (TS - 1) * TS + line_at,
        jnp.where(line_edge == 1, line_at * TS + TS - 1, jnp.where(line_edge == 2, line_at, line_at * TS)),
    )
    place_ref[...] = (iota((LANES, CELLS), 1) == rim_cell).astype(F32).astype(BF16)

    for copy, (k, _) in zip(copies, spans):
        copy.wait()
        part = dot(chosen[:, k : k + CHUNK], streamed[k : k + CHUNK])
        total = part if total is None else total + part
    scalars_ref[...] = total[WINDS:].astype(BF16)
    wind = total[:WINDS]
    wind_ref[...] = wind
    east, north = wind[:LEV], wind[LEV:]

    cell = iota((1, CELLS), 1)
    row, col = cell >> 5, cell & (TS - 1)
    trig = trig_ref[...]
    cosine, sine = trig[0:1], trig[1:2]
    ex, exm, ey, eym = neighbours_within(east, row, col)
    nx, nxm, ny, nym = neighbours_within(north, row, col)
    curl = cosine * (0.5 * (nx - nxm) - 0.5 * (ey - eym)) - sine * (0.5 * (ex - exm) + 0.5 * (ny - nym))

    hi, lo = halves(jnp.concatenate([east, north, curl, trig], axis=0))
    both = jnp.concatenate([hi, lo], axis=0)
    got = dot(both.astype(BF16), pick_ref[...])

    lane = iota((LEV, LANES), 1)
    level = iota((LEV, LANES), 0)
    group = lane >> 5
    corners = got[:, LANES:]
    common_top = jnp.where((level == 5) | (level == 6), corners[24:32], 0.0)
    for e in range(4):
        tile = meta[1, e].astype(F32)
        code = (meta[2, e] * 2 + meta[3, e]).astype(F32)
        common_top = jnp.where((level == 4) & (lane == 96 + e), tile, common_top)
        common_top = jnp.where((level == 4) & (lane == 100 + e), code, common_top)
    common_low = jnp.where(
        lane >= 112, corners[8:16], jnp.where((lane & 3) == 3, corners[16:24], corners[0:8])
    )
    common_low = jnp.where(group == 3, common_low, 0.0)
    common = jnp.concatenate([common_top, common_low], axis=0).astype(BF16)
    for t in range(TILES):
        send_ref[t] = common
    sources = [
        (both[:, CELLS - LANES :], 96, 64),
        (got[:, :LANES], 0, 32),
        (both[:, :LANES], 0, 32),
        (got[:, :LANES], 64, 96),
    ]
    for e, (rim, at0, at1) in enumerate(sources):

        def to(goal, rows, start):
            return rim[rows] if goal == start else roll(rim[rows], goal - start)

        east_rows, north_rows, curl_rows, trig_rows = (slice(8 * i, 8 * i + 8) for i in range(4))
        east_low, north_low = slice(32, 40), slice(40, 48)
        top = jnp.where(group == 2, to(64, curl_rows, at0), common_top)
        top = jnp.where(group == 0, to(0, east_rows, at0), jnp.where(group == 1, to(32, east_low, at0), top))
        top = jnp.where((group == 3) & (level < 2), to(96, trig_rows, at0), top)
        top = jnp.where((group == 3) & ((level == 2) | (level == 3)), to(96, trig_rows, at1), top)
        low = jnp.where(group == 2, to(64, curl_rows, at1), common_low)
        low = jnp.where(group == 0, to(0, north_rows, at0), jnp.where(group == 1, to(32, north_low, at0), low))
        send_ref[slot(meta[1, e])] = jnp.concatenate([top, low], axis=0).astype(BF16)


def smooth_kernel(
    meta_ref, packets_ref, wind_ref, trig_ref, place_ref, scalars_ref, scalars_out_ref, dgrid_ref, vortex_ref
):
    meta = meta_ref[...]

    def packet(tile):
        both = packets_ref[slot(tile)].astype(F32)
        return both[:LEV], both[LEV:]

    def corner_of(edge, end):
        return jnp.where((edge & 1) == 0, jnp.where(edge == 0, 2, 0) + end, 2 * end + jnp.where(edge == 1, 1, 0))

    scalars_out_ref[...] = scalars_ref[...]
    lane = iota((LEV, LANES), 1)
    group = lane >> 5
    at = lane & 31
    zero = jnp.zeros((LEV, LANES), F32)
    edges = [meta[2, e] for e in range(4)]
    near = [packet(meta[1, e]) for e in range(4)]

    def code_of(top, edge):
        codes = pltpu.roll(top * 8.0 + roll(top, -4), (LANES - 96 - edge) & 127, 1)
        return codes[4, 0].astype(jnp.int32)

    def strip(half, source):
        out = roll(near[0][half], -32 * source)
        for e in range(1, 4):
            out = jnp.where(group == e, roll(near[e][half], 32 * (e - source)), out)
        return out

    east_hi, east_lo, c0, misc = [strip(0, s) for s in range(4)]
    north_hi, north_lo, c1 = [strip(1, s) for s in range(3)]
    east0, north0 = east_hi + east_lo, north_hi + north_lo
    cos0, sin0, cos1, sin1 = [misc[r : r + 1] for r in range(4)]
    lane1 = iota((1, LANES), 1)
    edge_of = lane_pick(lane1 >> 5, edges)

    spots = [(e, end) for e in range(4) for end in range(2)]

    def take(into, vector, source, spot):
        goal = 32 * spot[0] + 31 * spot[1]
        return jnp.where(lane == goal, pltpu.roll(vector, (goal + LANES - source) & 127, 1), into)

    def mark(into, value, spot):
        return jnp.where(lane1 == 32 * spot[0] + 31 * spot[1], value, into)

    own_qe, own_qn = zero, zero
    side_v = jnp.zeros((1, LANES), jnp.int32)
    sides = []
    for spot in spots:
        e, end = spot
        even = (edges[e] & 1) == 0
        side = jnp.where(even, 1 if end else 3, 0 if end else 2)
        corner = corner_of(edges[e], end)
        beside = jnp.where(even, 2, 1)
        own_qe = take(own_qe, near[e][1], 96 + 4 * corner + beside, spot)
        own_qn = take(own_qn, near[e][1], 112 + 4 * corner + beside, spot)
        side_v = mark(side_v, side, spot)
        sides.append(side)

    far = []
    for spot, side in zip(spots, sides):
        code = code_of(near[spot[0]][0], side)
        end = (edges[spot[0]] < 2).astype(jnp.int32) ^ (code & 1)
        far.append((packet(code >> 3), (code >> 1) & 3, end))

    far_e, far_n, far_qe, far_qn, far_c, far_cos, far_sin = (zero,) * 7
    far_edge_v, far_side_v = jnp.zeros_like(side_v), jnp.zeros_like(side_v)
    sides = []
    for spot, ((top, low), edge, end) in zip(spots, far):
        corner = corner_of(edge, end)
        even = (edge & 1) == 0
        beside = jnp.where(even, 1, 2)
        side = jnp.where(even, jnp.where(end == 1, 1, 3), jnp.where(end == 1, 0, 2))
        far_e = take(far_e, low, 96 + 4 * corner, spot)
        far_n = take(far_n, low, 112 + 4 * corner, spot)
        far_qe = take(far_qe, low, 96 + 4 * corner + beside, spot)
        far_qn = take(far_qn, low, 112 + 4 * corner + beside, spot)
        far_c = take(far_c, low, 96 + 4 * corner + 3, spot)
        trig = take(zero, top, 96 + 4 * corner, spot)
        far_cos, far_sin = far_cos + trig[6:7], far_sin + trig[5:6]
        far_edge_v = mark(far_edge_v, edge, spot)
        far_side_v = mark(far_side_v, side, spot)
        sides.append(side)

    place = place_ref[...]
    cell = iota((1, CELLS), 1)
    row, col = cell >> 5, cell & (TS - 1)
    along_x = (group & 1) == 1

    def rims_of(fields):
        hi, lo = halves(fields)
        got = dot(jnp.concatenate([hi, lo], axis=0).astype(BF16), place, ((1,), (1,)))
        return got[: fields.shape[0]] + got[fields.shape[0] :]

    def placed(pairs):
        parts = [p for pair in pairs for p in pair]
        parts = [jnp.where(along_x, p, 0.0) for p in parts] + [jnp.where(along_x, 0.0, p) for p in parts]
        got = dot(jnp.concatenate(parts, axis=0).astype(BF16), place)
        got = [got[LEV * i : LEV * (i + 1)] for i in range(len(parts))]
        got = [got[i] + got[i + 1] for i in range(0, len(got), 2)]
        return [(got[i], got[i + len(pairs)]) for i in range(len(pairs))]

    def shifts(h, halo):
        halo_x, halo_y = halo
        return (
            jnp.where(col == TS - 1, halo_x, roll(h, -1)),
            jnp.where(col == 0, halo_x, roll(h, 1)),
            jnp.where(row == TS - 1, halo_y, roll(h, -TS)),
            jnp.where(row == 0, halo_y, roll(h, TS)),
        )

    wind = wind_ref[...]
    east, north = wind[:LEV], wind[LEV:]
    cosine, sine = trig_ref[0:1, :], trig_ref[1:2, :]
    rim = rims_of(wind)
    rim_e, rim_n = rim[:LEV], rim[LEV:]

    c0 = c0 + towards(edge_of, cos0, sin0, rim_e - east0, rim_n - north0)
    ends = (at == 0) | (at == 31)
    c0 = c0 + jnp.where(ends, towards(side_v, cos0, sin0, far_e - east0, far_n - north0), 0.0)
    c1 = c1 + jnp.where(ends, towards(side_v, cos1, sin1, far_qe - own_qe, far_qn - own_qn), 0.0)
    far_c = far_c + towards(far_edge_v, far_cos, far_sin, east0 - far_e, north0 - far_n)

    last_e, last_n = zero, zero
    for index, (spot, side) in enumerate(zip(spots, sides)):
        code = code_of(far[index][0][0], side)
        end = (far[index][1] < 2).astype(jnp.int32) ^ (code & 1)
        corner = corner_of((code >> 1) & 3, end)
        _, low = packet(code >> 3)
        last_e = take(last_e, low, 96 + 4 * corner, spot)
        last_n = take(last_n, low, 112 + 4 * corner, spot)
    far_c = far_c + towards(far_side_v, far_cos, far_sin, last_e - far_e, last_n - far_n)
    after = jnp.where(at == 31, far_c, roll(c0, -1))
    before = jnp.where(at == 0, far_c, roll(c0, 1))
    s0 = c0 + 0.2 * (c1 + after + before - 4.0 * c0)
    halo_e, halo_n = placed([(east_hi, east_lo), (north_hi, north_lo)])
    halo_c, halo_s = placed([halves(c0), halves(s0)])

    ex, exm, ey, eym = shifts(east, halo_e)
    nx, nxm, ny, nym = shifts(north, halo_n)
    along = cosine * (0.5 * (east + ey)) + sine * (0.5 * (north + ny))
    across = -sine * (0.5 * (east + ex)) + cosine * (0.5 * (north + nx))
    dgrid_ref[...] = jnp.concatenate([along, across], axis=0).astype(BF16)
    vortex = cosine * (0.5 * (nx - nxm) - 0.5 * (ey - eym)) - sine * (0.5 * (ex - exm) + 0.5 * (ny - nym))
    halo_s = tuple(h + 0.2 * vortex for h in halo_s)
    for halo in (halo_c, halo_s):
        xp, xm, yp, ym = shifts(vortex, halo)
        vortex = vortex + 0.2 * (xp + xm + yp + ym - 4.0 * vortex)
    vortex_ref[...] = vortex


def vmem():
    return pl.BlockSpec(memory_space=pltpu.VMEM)


def shape(dims, kind):
    return jax.ShapeDtypeStruct(dims, kind)


def hbm():
    return pl.BlockSpec(memory_space=pltpu.HBM)


def cost(flops, moved):
    return pl.CostEstimate(flops=flops, bytes_accessed=moved, transcendentals=0)


def body(checkpoint, remap_weights, margins, seams, rotation_angle):
    weights = remap_weights[0, 0].reshape(K * SB, CELLS)
    limit = pltpu.CompilerParams(vmem_limit_bytes=16 * MIB)

    def in_hbm(x):
        return pltpu.with_memory_space_constraint(x, pltpu.HBM)

    asked, meta, held = pl.pallas_call(
        ask_kernel,
        out_shape=(
            shape((N_TILE, 1, LANES), jnp.int32),
            shape((LEV, LANES), jnp.int32),
            shape(checkpoint.shape, BF16),
        ),
        in_specs=[hbm()] * 3,
        out_specs=(vmem(),) * 3,
        scratch_shapes=[
            pltpu.SMEM((K,), jnp.int32),
            pltpu.SMEM((3, 1, 4), jnp.int32),
            pltpu.SemaphoreType.DMA((3,)),
        ],
        compiler_params=limit,
        name="ask",
    )(in_hbm(margins[0, 0]), in_hbm(seams.reshape(3, 1, 4)), in_hbm(checkpoint))
    asked = lax.all_to_all(asked, "tile", 0, 0, tiled=True).reshape(N_TILE, LANES)
    blocks = pl.pallas_call(
        select_kernel,
        out_shape=shape((N_TILE, ROWS, CAP * SB), BF16),
        in_specs=[vmem(), vmem()],
        out_specs=vmem(),
        compiler_params=limit,
        name="select",
    )(asked, held)
    blocks = lax.all_to_all(blocks, "tile", 0, 0, tiled=True)

    scalars, wind, trig, place, packets = pl.pallas_call(
        remap_kernel,
        out_shape=(
            shape((ROWS - WINDS, CELLS), BF16),
            shape((WINDS, CELLS), F32),
            shape((LEV, CELLS), F32),
            shape((LANES, CELLS), BF16),
            shape((TILES, 16, LANES), BF16),
        ),
        in_specs=[vmem(), vmem(), hbm(), hbm()],
        out_specs=(vmem(),) * 5,
        scratch_shapes=[
            pltpu.VMEM((ROWS, K * SB), BF16),
            pltpu.VMEM((K * SB, CELLS), BF16),
            pltpu.VMEM((CELLS, 2 * LANES), BF16),
            pltpu.VMEM((1, CELLS), F32),
            pltpu.SemaphoreType.DMA((K * SB // CHUNK + 1,)),
        ],
        compiler_params=limit,
        cost_estimate=cost(2 * ROWS * K * SB * CELLS, 9 * MIB),
        name="remap",
    )(meta, blocks, in_hbm(weights), in_hbm(rotation_angle[0, 0].reshape(1, CELLS)))
    packets = lax.all_to_all(
        packets, ("face", "tile"), 0, 0, axis_index_groups=[sorted(range(TILES), key=slot_bits)], tiled=True
    )

    scalars, dgrid, vortex = pl.pallas_call(
        smooth_kernel,
        out_shape=(
            shape((ROWS - WINDS, CELLS), BF16),
            shape((WINDS, CELLS), BF16),
            shape((LEV, CELLS), F32),
        ),
        in_specs=[vmem()] * 6,
        out_specs=(vmem(),) * 3,
        compiler_params=limit,
        name="smooth",
    )(meta, packets, wind, trig, place, scalars)
    return (
        scalars.reshape(1, 1, ROWS - WINDS, CELLS),
        dgrid.reshape(1, 1, WINDS, CELLS),
        vortex.reshape(1, 1, LEV, CELLS),
    )


def solution(mesh):
    placed = (
        P(None, "tile"),
        P("face", "tile", None, None, None),
        P("face", "tile", None),
        P("face", "tile", None, None),
        P("face", "tile", None),
    )
    return jax.shard_map(
        body,
        mesh=mesh,
        in_specs=placed,
        out_specs=(P("face", "tile", None, None),) * 3,
        check_vma=False,
    )
```

```python
import jax
import jax.numpy as jnp
from jax import lax
from jax.experimental import pallas as pl
from jax.experimental.pallas import tpu as pltpu
from jax.sharding import PartitionSpec as P

LEV = 8
FIELDS = 6
TS = 32
CELLS = TS * TS
SB = 256
BLK_DEV = 8
K = 16
CAP = 2
GROUPS = K // CAP
N_TILE = 16
TILES = 128
ROWS = FIELDS * LEV
WINDS = 2 * LEV
LANES = 128
MIB = 1 << 20
CHUNK = 256
F32 = jnp.float32
BF16 = jnp.bfloat16


def iota(shape, dim):
    return lax.broadcasted_iota(jnp.int32, shape, dim)


def dot(a, b, contract=((1,), (0,))):
    return lax.dot_general(a, b, (contract, ((), ())), preferred_element_type=F32)


def halves(x):
    hi = x.astype(BF16).astype(F32)
    return hi, x - hi


def roll(x, shift):
    return pltpu.roll(x, shift % x.shape[1], 1)


def lane_pick(group, values):
    out = jnp.full(group.shape, values[0])
    for index in range(1, len(values)):
        out = jnp.where(group == index, values[index], out)
    return out


def towards(direction, cosine, sine, d_east, d_north):
    a_east = jnp.where(
        direction == 0, -cosine, jnp.where(direction == 1, -sine, jnp.where(direction == 2, cosine, sine))
    )
    a_north = jnp.where(
        direction == 0, -sine, jnp.where(direction == 1, cosine, jnp.where(direction == 2, sine, -cosine))
    )
    return 0.5 * (a_east * d_east + a_north * d_north)


def neighbours_within(h, row, col):
    return (
        jnp.where(col == TS - 1, h, roll(h, -1)),
        jnp.where(col == 0, h, roll(h, 1)),
        jnp.where(row == TS - 1, h, roll(h, -TS)),
        jnp.where(row == 0, h, roll(h, TS)),
    )


def ask_kernel(
    margins_ref, seams_ref, checkpoint_ref, asked_ref, meta_ref, held_ref, margins, seams, sems
):
    copies = [
        pltpu.make_async_copy(margins_ref, margins, sems.at[0]),
        pltpu.make_async_copy(seams_ref, seams, sems.at[1]),
        pltpu.make_async_copy(checkpoint_ref, held_ref, sems.at[2]),
    ]
    for copy in copies:
        copy.start()
    copies[0].wait()
    reader, lane = iota((N_TILE, LANES), 0), iota((N_TILE, LANES), 1)
    asked = jnp.zeros((N_TILE, LANES), jnp.int32)
    for m in range(GROUPS):
        first, second = margins[CAP * m], margins[CAP * m + 1]
        asked = jnp.where(reader == (first >> 3), jnp.where(lane == 0, first, second), asked)
    asked = asked & (BLK_DEV - 1)
    for r in range(N_TILE):
        asked_ref[r] = asked[r : r + 1]

    copies[1].wait()
    level, lane = iota((LEV, LANES), 0), iota((LEV, LANES), 1)
    meta = jnp.zeros((LEV, LANES), jnp.int32)
    for m in range(GROUPS):
        reader = jnp.clip(margins[CAP * m] >> 3, 0, N_TILE - 1)
        meta = jnp.where((level == 0) & (lane == m), reader, meta)
    for kind in range(3):
        for e in range(4):
            meta = jnp.where((level == kind + 1) & (lane == e), seams[kind, 0, e], meta)
    meta_ref[...] = meta
    copies[2].wait()


def slot(tile):
    tile = jnp.clip(tile, 0, TILES - 1)
    return (tile & (N_TILE - 1)) * (TILES // N_TILE) + (tile >> 4)


def select_kernel(asked_ref, held_ref, out_ref):
    asked = asked_ref[...]
    for g in range(N_TILE):
        for j in range(CAP):
            block = asked[g, j] & (BLK_DEV - 1)
            out_ref[g, :, j * SB : (j + 1) * SB] = held_ref[:, pl.ds(pl.multiple_of(block * SB, SB), SB)]


def remap_kernel(
    meta_ref, blocks_ref, weights_ref, angle_ref,
    scalars_ref, wind_ref, trig_ref, place_ref, send_ref,
    chosen, streamed, pick_ref, angle, sems,
):
    angle_copy = pltpu.make_async_copy(angle_ref, angle, sems.at[K * SB // CHUNK])
    angle_copy.start()
    spans = [(k, pl.ds(k, CHUNK)) for k in range(0, K * SB, CHUNK)]
    copies = [
        pltpu.make_async_copy(weights_ref.at[span], streamed.at[span], sems.at[index])
        for index, (k, span) in enumerate(spans)
    ]
    for copy in copies:
        copy.start()
    meta = meta_ref[...]
    for m in range(GROUPS):
        chosen[:, CAP * SB * m : CAP * SB * (m + 1)] = blocks_ref[meta[0, m]]
    total = None

    angle_copy.wait()
    trig_ref[...] = jnp.where((iota((LEV, CELLS), 0) & 1) == 0, jnp.cos(angle[...]), jnp.sin(angle[...]))

    lane = iota((1, 2 * LANES), 1)
    depth, at = (lane >> 5) & 1, lane & 31
    column_cell = at * TS + jnp.where((lane >> 6) == 0, TS - 1 - depth, depth)
    corner, k = (lane >> 2) & 3, lane & 3
    c_row, c_col = (corner >> 1) * (TS - 1), (corner & 1) * (TS - 1)
    c_row = jnp.where(k == 2, jnp.where(c_row == 0, 1, TS - 2), c_row)
    c_col = jnp.where(k == 1, jnp.where(c_col == 0, 1, TS - 2), c_col)
    corner_cell = jnp.where((lane & 127) >= 96, c_row * TS + c_col, -1)
    taken = jnp.where(lane < LANES, column_cell, corner_cell)
    pick_ref[...] = (iota((CELLS, 2 * LANES), 0) == taken).astype(F32).astype(BF16)

    line = iota((LANES, 1), 0)
    line_edge, line_at = line >> 5, line & 31
    flipped = lane_pick(line_edge, [meta[3, e] for e in range(4)]) == 1
    line_at = jnp.where(flipped, TS - 1 - line_at, line_at)
    rim_cell = jnp.where(
        line_edge == 0, (TS - 1) * TS + line_at,
        jnp.where(line_edge == 1, line_at * TS + TS - 1, jnp.where(line_edge == 2, line_at, line_at * TS)),
    )
    place_ref[...] = (iota((LANES, CELLS), 1) == rim_cell).astype(F32).astype(BF16)

    for copy, (k, _) in zip(copies, spans):
        copy.wait()
        part = dot(chosen[:, k : k + CHUNK], streamed[k : k + CHUNK])
        total = part if total is None else total + part
    scalars_ref[...] = total[WINDS:].astype(BF16)
    wind = total[:WINDS]
    wind_ref[...] = wind
    east, north = wind[:LEV], wind[LEV:]

    cell = iota((1, CELLS), 1)
    row, col = cell >> 5, cell & (TS - 1)
    trig = trig_ref[...]
    cosine, sine = trig[0:1], trig[1:2]
    ex, exm, ey, eym = neighbours_within(east, row, col)
    nx, nxm, ny, nym = neighbours_within(north, row, col)
    curl = cosine * (0.5 * (nx - nxm) - 0.5 * (ey - eym)) - sine * (0.5 * (ex - exm) + 0.5 * (ny - nym))

    hi, lo = halves(jnp.concatenate([east, north, curl, trig], axis=0))
    both = jnp.concatenate([hi, lo], axis=0)
    got = dot(both.astype(BF16), pick_ref[...])

    lane = iota((LEV, LANES), 1)
    level = iota((LEV, LANES), 0)
    group = lane >> 5
    corners = got[:, LANES:]
    common_top = jnp.where((level == 5) | (level == 6), corners[24:32], 0.0)
    for e in range(4):
        tile = meta[1, e].astype(F32)
        code = (meta[2, e] * 2 + meta[3, e]).astype(F32)
        common_top = jnp.where((level == 4) & (lane == 96 + e), tile, common_top)
        common_top = jnp.where((level == 4) & (lane == 100 + e), code, common_top)
    common_low = jnp.where(
        lane >= 112, corners[8:16], jnp.where((lane & 3) == 3, corners[16:24], corners[0:8])
    )
    common_low = jnp.where(group == 3, common_low, 0.0)
    common = jnp.concatenate([common_top, common_low], axis=0).astype(BF16)
    for t in range(TILES):
        send_ref[t] = common
    sources = [
        (both[:, CELLS - LANES :], 96, 64),
        (got[:, :LANES], 0, 32),
        (both[:, :LANES], 0, 32),
        (got[:, :LANES], 64, 96),
    ]
    for e, (rim, at0, at1) in enumerate(sources):

        def to(goal, rows, start):
            return rim[rows] if goal == start else roll(rim[rows], goal - start)

        east_rows, north_rows, curl_rows, trig_rows = (slice(8 * i, 8 * i + 8) for i in range(4))
        east_low, north_low = slice(32, 40), slice(40, 48)
        top = jnp.where(group == 2, to(64, curl_rows, at0), common_top)
        top = jnp.where(group == 0, to(0, east_rows, at0), jnp.where(group == 1, to(32, east_low, at0), top))
        top = jnp.where((group == 3) & (level < 2), to(96, trig_rows, at0), top)
        top = jnp.where((group == 3) & ((level == 2) | (level == 3)), to(96, trig_rows, at1), top)
        low = jnp.where(group == 2, to(64, curl_rows, at1), common_low)
        low = jnp.where(group == 0, to(0, north_rows, at0), jnp.where(group == 1, to(32, north_low, at0), low))
        send_ref[slot(meta[1, e])] = jnp.concatenate([top, low], axis=0).astype(BF16)


def smooth_kernel(
    meta_ref, packets_ref, wind_ref, trig_ref, place_ref, scalars_ref, scalars_out_ref, dgrid_ref, vortex_ref
):
    meta = meta_ref[...]

    def packet(tile):
        both = packets_ref[slot(tile)].astype(F32)
        return both[:LEV], both[LEV:]

    def corner_of(edge, end):
        return jnp.where((edge & 1) == 0, jnp.where(edge == 0, 2, 0) + end, 2 * end + jnp.where(edge == 1, 1, 0))

    scalars_out_ref[...] = scalars_ref[...]
    lane = iota((LEV, LANES), 1)
    group = lane >> 5
    at = lane & 31
    zero = jnp.zeros((LEV, LANES), F32)
    edges = [meta[2, e] for e in range(4)]
    near = [packet(meta[1, e]) for e in range(4)]

    def code_of(top, edge):
        codes = pltpu.roll(top * 8.0 + roll(top, -4), (LANES - 96 - edge) & 127, 1)
        return codes[4, 0].astype(jnp.int32)

    def strip(half, source):
        out = roll(near[0][half], -32 * source)
        for e in range(1, 4):
            out = jnp.where(group == e, roll(near[e][half], 32 * (e - source)), out)
        return out

    east_hi, east_lo, c0, misc = [strip(0, s) for s in range(4)]
    north_hi, north_lo, c1 = [strip(1, s) for s in range(3)]
    east0, north0 = east_hi + east_lo, north_hi + north_lo
    cos0, sin0, cos1, sin1 = [misc[r : r + 1] for r in range(4)]
    lane1 = iota((1, LANES), 1)
    edge_of = lane_pick(lane1 >> 5, edges)

    spots = [(e, end) for e in range(4) for end in range(2)]

    def take(into, vector, source, spot):
        goal = 32 * spot[0] + 31 * spot[1]
        return jnp.where(lane == goal, pltpu.roll(vector, (goal + LANES - source) & 127, 1), into)

    def mark(into, value, spot):
        return jnp.where(lane1 == 32 * spot[0] + 31 * spot[1], value, into)

    own_qe, own_qn = zero, zero
    side_v = jnp.zeros((1, LANES), jnp.int32)
    sides = []
    for spot in spots:
        e, end = spot
        even = (edges[e] & 1) == 0
        side = jnp.where(even, 1 if end else 3, 0 if end else 2)
        corner = corner_of(edges[e], end)
        beside = jnp.where(even, 2, 1)
        own_qe = take(own_qe, near[e][1], 96 + 4 * corner + beside, spot)
        own_qn = take(own_qn, near[e][1], 112 + 4 * corner + beside, spot)
        side_v = mark(side_v, side, spot)
        sides.append(side)

    far = []
    for spot, side in zip(spots, sides):
        code = code_of(near[spot[0]][0], side)
        end = (edges[spot[0]] < 2).astype(jnp.int32) ^ (code & 1)
        far.append((packet(code >> 3), (code >> 1) & 3, end))

    far_e, far_n, far_qe, far_qn, far_c, far_cos, far_sin = (zero,) * 7
    far_edge_v, far_side_v = jnp.zeros_like(side_v), jnp.zeros_like(side_v)
    sides = []
    for spot, ((top, low), edge, end) in zip(spots, far):
        corner = corner_of(edge, end)
        even = (edge & 1) == 0
        beside = jnp.where(even, 1, 2)
        side = jnp.where(even, jnp.where(end == 1, 1, 3), jnp.where(end == 1, 0, 2))
        far_e = take(far_e, low, 96 + 4 * corner, spot)
        far_n = take(far_n, low, 112 + 4 * corner, spot)
        far_qe = take(far_qe, low, 96 + 4 * corner + beside, spot)
        far_qn = take(far_qn, low, 112 + 4 * corner + beside, spot)
        far_c = take(far_c, low, 96 + 4 * corner + 3, spot)
        trig = take(zero, top, 96 + 4 * corner, spot)
        far_cos, far_sin = far_cos + trig[6:7], far_sin + trig[5:6]
        far_edge_v = mark(far_edge_v, edge, spot)
        far_side_v = mark(far_side_v, side, spot)
        sides.append(side)

    place = place_ref[...]
    cell = iota((1, CELLS), 1)
    row, col = cell >> 5, cell & (TS - 1)
    along_x = (group & 1) == 1

    def rims_of(fields):
        hi, lo = halves(fields)
        got = dot(jnp.concatenate([hi, lo], axis=0).astype(BF16), place, ((1,), (1,)))
        return got[: fields.shape[0]] + got[fields.shape[0] :]

    def placed(pairs):
        parts = [p for pair in pairs for p in pair]
        parts = [jnp.where(along_x, p, 0.0) for p in parts] + [jnp.where(along_x, 0.0, p) for p in parts]
        got = dot(jnp.concatenate(parts, axis=0).astype(BF16), place)
        got = [got[LEV * i : LEV * (i + 1)] for i in range(len(parts))]
        got = [got[i] + got[i + 1] for i in range(0, len(got), 2)]
        return [(got[i], got[i + len(pairs)]) for i in range(len(pairs))]

    def shifts(h, halo):
        halo_x, halo_y = halo
        return (
            jnp.where(col == TS - 1, halo_x, roll(h, -1)),
            jnp.where(col == 0, halo_x, roll(h, 1)),
            jnp.where(row == TS - 1, halo_y, roll(h, -TS)),
            jnp.where(row == 0, halo_y, roll(h, TS)),
        )

    wind = wind_ref[...]
    east, north = wind[:LEV], wind[LEV:]
    cosine, sine = trig_ref[0:1, :], trig_ref[1:2, :]
    rim = rims_of(wind)
    rim_e, rim_n = rim[:LEV], rim[LEV:]

    c0 = c0 + towards(edge_of, cos0, sin0, rim_e - east0, rim_n - north0)
    ends = (at == 0) | (at == 31)
    c0 = c0 + jnp.where(ends, towards(side_v, cos0, sin0, far_e - east0, far_n - north0), 0.0)
    c1 = c1 + jnp.where(ends, towards(side_v, cos1, sin1, far_qe - own_qe, far_qn - own_qn), 0.0)
    far_c = far_c + towards(far_edge_v, far_cos, far_sin, east0 - far_e, north0 - far_n)

    last_e, last_n = zero, zero
    for index, (spot, side) in enumerate(zip(spots, sides)):
        code = code_of(far[index][0][0], side)
        end = (far[index][1] < 2).astype(jnp.int32) ^ (code & 1)
        corner = corner_of((code >> 1) & 3, end)
        _, low = packet(code >> 3)
        last_e = take(last_e, low, 96 + 4 * corner, spot)
        last_n = take(last_n, low, 112 + 4 * corner, spot)
    far_c = far_c + towards(far_side_v, far_cos, far_sin, last_e - far_e, last_n - far_n)
    after = jnp.where(at == 31, far_c, roll(c0, -1))
    before = jnp.where(at == 0, far_c, roll(c0, 1))
    s0 = c0 + 0.2 * (c1 + after + before - 4.0 * c0)
    halo_e, halo_n = placed([(east_hi, east_lo), (north_hi, north_lo)])
    (halo_c,) = placed([halves(c0)])
    (halo_s,) = placed([halves(s0)])

    ex, exm, ey, eym = shifts(east, halo_e)
    nx, nxm, ny, nym = shifts(north, halo_n)
    along = cosine * (0.5 * (east + ey)) + sine * (0.5 * (north + ny))
    across = -sine * (0.5 * (east + ex)) + cosine * (0.5 * (north + nx))
    dgrid_ref[...] = jnp.concatenate([along, across], axis=0).astype(BF16)
    vortex = cosine * (0.5 * (nx - nxm) - 0.5 * (ey - eym)) - sine * (0.5 * (ex - exm) + 0.5 * (ny - nym))
    halo_s = tuple(h + 0.2 * vortex for h in halo_s)
    for halo in (halo_c, halo_s):
        xp, xm, yp, ym = shifts(vortex, halo)
        vortex = vortex + 0.2 * (xp + xm + yp + ym - 4.0 * vortex)
    vortex_ref[...] = vortex


def vmem():
    return pl.BlockSpec(memory_space=pltpu.VMEM)


def shape(dims, kind):
    return jax.ShapeDtypeStruct(dims, kind)


def hbm():
    return pl.BlockSpec(memory_space=pltpu.HBM)


def cost(flops, moved):
    return pl.CostEstimate(flops=flops, bytes_accessed=moved, transcendentals=0)


def body(checkpoint, remap_weights, margins, seams, rotation_angle):
    weights = remap_weights[0, 0].reshape(K * SB, CELLS)
    limit = pltpu.CompilerParams(vmem_limit_bytes=16 * MIB)

    def in_hbm(x):
        return pltpu.with_memory_space_constraint(x, pltpu.HBM)

    asked, meta, held = pl.pallas_call(
        ask_kernel,
        out_shape=(
            shape((N_TILE, 1, LANES), jnp.int32),
            shape((LEV, LANES), jnp.int32),
            shape(checkpoint.shape, BF16),
        ),
        in_specs=[hbm()] * 3,
        out_specs=(vmem(),) * 3,
        scratch_shapes=[
            pltpu.SMEM((K,), jnp.int32),
            pltpu.SMEM((3, 1, 4), jnp.int32),
            pltpu.SemaphoreType.DMA((3,)),
        ],
        compiler_params=limit,
        name="ask",
    )(in_hbm(margins[0, 0]), in_hbm(seams.reshape(3, 1, 4)), in_hbm(checkpoint))
    asked = lax.all_to_all(asked, "tile", 0, 0, tiled=True).reshape(N_TILE, LANES)
    blocks = pl.pallas_call(
        select_kernel,
        out_shape=shape((N_TILE, ROWS, CAP * SB), BF16),
        in_specs=[vmem(), vmem()],
        out_specs=vmem(),
        compiler_params=limit,
        name="select",
    )(asked, held)
    blocks = lax.all_to_all(blocks, "tile", 0, 0, tiled=True)

    scalars, wind, trig, place, packets = pl.pallas_call(
        remap_kernel,
        out_shape=(
            shape((ROWS - WINDS, CELLS), BF16),
            shape((WINDS, CELLS), F32),
            shape((LEV, CELLS), F32),
            shape((LANES, CELLS), BF16),
            shape((TILES, 16, LANES), BF16),
        ),
        in_specs=[vmem(), vmem(), hbm(), hbm()],
        out_specs=(vmem(),) * 5,
        scratch_shapes=[
            pltpu.VMEM((ROWS, K * SB), BF16),
            pltpu.VMEM((K * SB, CELLS), BF16),
            pltpu.VMEM((CELLS, 2 * LANES), BF16),
            pltpu.VMEM((1, CELLS), F32),
            pltpu.SemaphoreType.DMA((K * SB // CHUNK + 1,)),
        ],
        compiler_params=limit,
        cost_estimate=cost(2 * ROWS * K * SB * CELLS, 9 * MIB),
        name="remap",
    )(meta, blocks, in_hbm(weights), in_hbm(rotation_angle[0, 0].reshape(1, CELLS)))
    packets = lax.all_to_all(packets, ("tile", "face"), 0, 0, tiled=True)

    scalars, dgrid, vortex = pl.pallas_call(
        smooth_kernel,
        out_shape=(
            shape((ROWS - WINDS, CELLS), BF16),
            shape((WINDS, CELLS), BF16),
            shape((LEV, CELLS), F32),
        ),
        in_specs=[vmem()] * 6,
        out_specs=(vmem(),) * 3,
        compiler_params=limit,
        name="smooth",
    )(meta, packets, wind, trig, place, scalars)
    return (
        scalars.reshape(1, 1, ROWS - WINDS, CELLS),
        dgrid.reshape(1, 1, WINDS, CELLS),
        vortex.reshape(1, 1, LEV, CELLS),
    )


def solution(mesh):
    placed = (
        P(None, "tile"),
        P("face", "tile", None, None, None),
        P("face", "tile", None),
        P("face", "tile", None, None),
        P("face", "tile", None),
    )
    return jax.shard_map(
        body,
        mesh=mesh,
        in_specs=placed,
        out_specs=(P("face", "tile", None, None),) * 3,
        check_vma=False,
    )
```
